256 devices in a mesh: pipe: 32 (over x_hi, z, core), tensor: 8 (over y, x_lo).
Axes of the slice: x: 4 (x_hi: 2, x_lo: 2; x = x_hi * 2 + x_lo), y: 4, z: 8, core: 2. Of those that a mesh axis runs over, the one named last changes fastest.
Arguments:
- saved: bfloat16 [32, 2, 128, 2560], P('pipe', None, 'tensor'), may hold values from -6 to 6
- cotangent: bfloat16 [32, 128, 2560], P('pipe', 'tensor'), may hold values from -6 to 6
- loss_grad: bfloat16 [128, 2560], P('tensor'), may hold values from -6 to 6
- lengths: int32 [32, 2], P('pipe'), may hold values from 32 to 128, as said below
- gain: float32 [32, 2560], P('pipe'), may hold values from 0.5 to 1.5
- w_query: bfloat16 [32, 2560, 2048], P('pipe', None, 'tensor'), may hold values from -0.19764235 to 0.19764235
- w_key: bfloat16 [32, 2560, 1024], P('pipe', None, 'tensor'), may hold values from -0.19764235 to 0.19764235
- w_value: bfloat16 [32, 2560, 1024], P('pipe', None, 'tensor'), may hold values from -0.125 to 0.125
- w_attn_out: bfloat16 [32, 2048, 2560], P('pipe', 'tensor'), may hold values from -0.125 to 0.125
- w_inner: bfloat16 [32, 2560, 4096], P('pipe', None, 'tensor'), may hold values from -0.125 to 0.125
- w_gate: bfloat16 [32, 2560, 4096], P('pipe', None, 'tensor'), may hold values from -0.125 to 0.125
- w_state: bfloat16 [32, 2560, 256], P('pipe'), may hold values from -0.125 to 0.125
- w_step: bfloat16 [32, 2560, 64], P('pipe', None, 'tensor'), may hold values from -0.125 to 0.125
- w_mamba_out: bfloat16 [32, 4096, 2560], P('pipe', 'tensor'), may hold values from -0.09375 to 0.09375
- conv_inner: bfloat16 [32, 4, 4096], P('pipe', None, 'tensor'), may hold values from -3 to 3
- conv_state: bfloat16 [32, 4, 256], P('pipe'), may hold values from -3 to 3
- step_bias: float32 [32, 64], P('pipe', 'tensor'), may hold values from -2 to 1
- decay_rate: float32 [32, 64], P('pipe', 'tensor'), may hold values from 0.003 to 0.5
Outputs:
- input_grad: bfloat16 [32, 128, 2560], P('pipe', 'tensor')
The draws below stay inside these ranges and needn't reach their ends.
Inputs may be any that keep to these rules, and one draw needn't show every extreme that they name: lengths[s, 1] equals lengths[s + 1, 0]: the second micro-batch of a section is the first one of the next section. The values 128 // 4 and 128 both occur.
All inputs are finite; a program needn't handle non-finite values.
Results may differ from the reference program's by a relative error of at most 0.02.
Values may be sent and summed in bfloat16 or wider, within the bound.
No kernel may reach another device: no remote copies, remote signals or barrier semaphores. Data moves between devices by JAX's collectives and lax.ppermute only.
A program may use at most 128 MiB of HBM per device.

```python
import math
import jax
import jax.numpy as jnp
from jax import lax

MODEL_WIDTH = 2560
QUERY_HEADS = 16
KEY_HEADS = 8
HEAD_SIZE = 128
MAMBA_HEADS = 64
MAMBA_HEAD = 64
STATE_SIZE = 128
CONV_TAPS = 4
TOKENS = 128
SECTIONS = 32


def draw_lengths(key, part):
    key = jax.random.fold_in(key, 11)
    base = jax.random.randint(key, (SECTIONS + 1,), TOKENS // 4, TOKENS + 1)
    spots = jax.random.permutation(jax.random.fold_in(key, 1), SECTIONS + 1)
    base = base.at[spots[0]].set(TOKENS).at[spots[1]].set(TOKENS // 4)
    return jnp.stack([base[:-1], base[1:]], axis=1).astype(jnp.int32)


def drawn_weight(key, heads):
    shape = (SECTIONS, MODEL_WIDTH, heads * HEAD_SIZE)
    factor = MODEL_WIDTH ** (-0.5)
    values = jax.random.truncated_normal(key, -4.0, 4.0, shape) * factor
    return values.astype(jnp.bfloat16)


def draw_w_query(key, part):
    key = jax.random.fold_in(key, 21)
    return drawn_weight(key, QUERY_HEADS)


def draw_w_key(key, part):
    key = jax.random.fold_in(key, 22)
    return drawn_weight(key, KEY_HEADS)


def steps_of(key, shape, pieces, low, top_value):
    loudness = 1.0
    for axis_at, blocks in pieces:
        steps = jax.random.uniform(jax.random.fold_in(jax.random.fold_in(key, 6), axis_at), (blocks,), jnp.float32, low / len(pieces), top_value / len(pieces))
        loudness = loudness * jnp.repeat(jnp.exp(steps), shape[axis_at] // blocks).reshape((-1,) + (1,) * (len(shape) - 1 - axis_at))
    return loudness


def normal_values(rng, extent, deviation, most, split=(), dtype=jnp.bfloat16):
    array = deviation * jax.random.normal(rng, extent, jnp.float32)
    if split:
        array = array * steps_of(rng, extent, split, -0.22, 0.18)
    return jnp.clip(array, -most, most).astype(dtype)


def setup_inputs(seed: int = 0) -> dict:
    arg_keys = jax.random.split(jax.random.key(seed), 19)
    return {
        "saved": normal_values(arg_keys[0], (SECTIONS, 2, TOKENS, MODEL_WIDTH), 1.0, 6.0, ((0, 32), (2, 8))),
        "cotangent": normal_values(arg_keys[1], (SECTIONS, TOKENS, MODEL_WIDTH), 1.0, 6.0, ((0, 32), (1, 8))),
        "loss_grad": normal_values(arg_keys[2], (TOKENS, MODEL_WIDTH), 1.0, 6.0, ((0, 8),)),
        "lengths": draw_lengths(jax.random.fold_in(arg_keys[18], 71), 0),
        "gain": jnp.clip(1.0 + 0.1 * jax.random.normal(arg_keys[4], (SECTIONS, MODEL_WIDTH), jnp.float32), 0.5, 1.5),
        "w_query": draw_w_query(jax.random.fold_in(arg_keys[18], 71), 0),
        "w_key": draw_w_key(jax.random.fold_in(arg_keys[18], 71), 0),
        "w_value": normal_values(arg_keys[7], (SECTIONS, MODEL_WIDTH, KEY_HEADS * HEAD_SIZE), MODEL_WIDTH ** -0.5, 0.125, ((0, 32), (2, 8))),
        "w_attn_out": normal_values(arg_keys[8], (SECTIONS, QUERY_HEADS * HEAD_SIZE, MODEL_WIDTH), (QUERY_HEADS * HEAD_SIZE) ** -0.5, 0.125, ((0, 32), (1, 8))),
        "w_inner": normal_values(arg_keys[9], (SECTIONS, MODEL_WIDTH, MAMBA_HEADS * MAMBA_HEAD), MODEL_WIDTH ** -0.5, 0.125, ((0, 32), (2, 8))),
        "w_gate": normal_values(arg_keys[10], (SECTIONS, MODEL_WIDTH, MAMBA_HEADS * MAMBA_HEAD), MODEL_WIDTH ** -0.5, 0.125, ((0, 32), (2, 8))),
        "w_state": normal_values(arg_keys[11], (SECTIONS, MODEL_WIDTH, 2 * STATE_SIZE), MODEL_WIDTH ** -0.5, 0.125, ((0, 32),)),
        "w_step": normal_values(arg_keys[12], (SECTIONS, MODEL_WIDTH, MAMBA_HEADS), MODEL_WIDTH ** -0.5, 0.125, ((0, 32), (2, 8))),
        "w_mamba_out": normal_values(arg_keys[13], (SECTIONS, MAMBA_HEADS * MAMBA_HEAD, MODEL_WIDTH), (MAMBA_HEADS * MAMBA_HEAD) ** -0.5, 0.09375, ((0, 32), (1, 8))),
        "conv_inner": normal_values(arg_keys[14], (SECTIONS, CONV_TAPS, MAMBA_HEADS * MAMBA_HEAD), 0.6, 3.0, ((0, 32), (2, 8))),
        "conv_state": normal_values(arg_keys[15], (SECTIONS, CONV_TAPS, 2 * STATE_SIZE), 0.6, 3.0, ((0, 32),)),
        "step_bias": jnp.clip(-2.0 + 3.0 * jax.random.uniform(arg_keys[16], (SECTIONS, MAMBA_HEADS), jnp.float32) ** steps_of(arg_keys[16], (SECTIONS, MAMBA_HEADS), ((0, 32), (1, 8)), -0.2, 0.2), -2.0, 1.0),
        "decay_rate": jnp.clip(jnp.exp(math.log(0.5) - 5.115996 * jax.random.uniform(arg_keys[17], (SECTIONS, MAMBA_HEADS), jnp.float32) ** steps_of(arg_keys[17], (SECTIONS, MAMBA_HEADS), ((0, 32), (1, 8)), -0.2, 0.2)), 0.003, 0.5),
    }


def row_scale(x):
    values = x.astype(jnp.float32)
    return lax.rsqrt(lax.optimization_barrier(jnp.mean(values * values, axis=-1, keepdims=True)) + 1e-05)

def normalize(x, gain):
    return (x.astype(jnp.float32) * row_scale(x) * gain).astype(jnp.bfloat16)

def norm_back(x, gain, d_normed):
    values = x.astype(jnp.float32)
    scale = row_scale(x)
    weighted = d_normed * gain
    return scale * weighted - values * (scale * scale * scale) * lax.optimization_barrier(jnp.mean(values * weighted, axis=-1, keepdims=True))

def causal_conv(values, taps):
    width = taps.shape[0]
    padded = jnp.pad(values, ((width - 1, 0), (0, 0)))
    total = jnp.zeros_like(values)
    for tap in range(width):
        total = total + padded[tap:tap + values.shape[0]] * taps[tap]
    return total

def mixer_core(query, key, value, inner, gate, state, raw_step, conv_inner, conv_state, step_bias, decay_rate, length):
    count = query.shape[0]
    heads_k = key.shape[1] // HEAD_SIZE
    group = query.shape[1] // key.shape[1]
    q_heads = query.reshape(count, heads_k, group, HEAD_SIZE)
    k_heads = key.reshape(count, heads_k, HEAD_SIZE)
    v_heads = value.reshape(count, heads_k, HEAD_SIZE)
    scores = jnp.einsum('tkgd,skd->kgts', q_heads, k_heads, preferred_element_type=jnp.float32) * HEAD_SIZE ** (-0.5)
    place = jnp.arange(count)
    causal = place[None, :] <= place[:, None]
    allowed = causal & (place[None, :] < length)
    scores = jnp.where(allowed, scores, -1e+30)
    top = lax.stop_gradient(lax.optimization_barrier(jnp.max(scores, axis=-1, keepdims=True)))
    expo = jnp.exp(scores - top)
    probs = (expo / lax.optimization_barrier(jnp.sum(expo, axis=-1, keepdims=True))).astype(jnp.bfloat16)
    attended = jnp.einsum('kgts,skd->tkgd', probs, v_heads, preferred_element_type=jnp.float32)
    attended = attended.astype(jnp.bfloat16).reshape(count, heads_k * group * HEAD_SIZE)
    heads_m = inner.shape[1] // MAMBA_HEAD
    mixed = jax.nn.silu(causal_conv(inner.astype(jnp.float32), conv_inner.astype(jnp.float32)))
    states = jax.nn.silu(causal_conv(state, conv_state.astype(jnp.float32)))
    b_in = states[:, :STATE_SIZE]
    c_out = states[:, STATE_SIZE:]
    step = jax.nn.softplus(raw_step + step_bias)
    total = jnp.cumsum(-step * decay_rate, axis=0)
    diffs = total[:, None, :] - total[None, :, :]
    decay = jnp.exp(jnp.where(causal[:, :, None], diffs, -1e+30))
    intersection = jnp.dot(c_out, b_in.T, precision=lax.Precision.HIGHEST)
    weight = intersection[:, :, None] * decay * step[None, :, :]
    mixed_heads = mixed.reshape(count, heads_m, MAMBA_HEAD)
    scan_out = jnp.einsum('trh,rhp->thp', weight, mixed_heads, precision=lax.Precision.HIGHEST)
    scan_out = scan_out + mixed_heads
    gated = scan_out * jax.nn.silu(gate.astype(jnp.float32)).reshape(count, heads_m, MAMBA_HEAD)
    return (attended, gated.astype(jnp.bfloat16).reshape(count, heads_m * MAMBA_HEAD))

def section_back(x, grad, length, params):
    gain, w_query, w_key, w_value, w_attn_out, w_inner, w_gate, w_state, w_step, w_mamba_out, conv_inner, conv_state, step_bias, decay_rate = params
    normed = normalize(x, gain)
    query = jnp.dot(normed, w_query, preferred_element_type=jnp.float32).astype(jnp.bfloat16)
    key = jnp.dot(normed, w_key, preferred_element_type=jnp.float32).astype(jnp.bfloat16)
    value = jnp.dot(normed, w_value, preferred_element_type=jnp.float32).astype(jnp.bfloat16)
    inner = jnp.dot(normed, w_inner, preferred_element_type=jnp.float32).astype(jnp.bfloat16)
    gate = jnp.dot(normed, w_gate, preferred_element_type=jnp.float32).astype(jnp.bfloat16)
    state = jnp.dot(normed, w_state, preferred_element_type=jnp.float32)
    raw_step = jnp.dot(normed, w_step, preferred_element_type=jnp.float32)
    d_attended = jnp.dot(grad, w_attn_out.T, preferred_element_type=jnp.float32).astype(jnp.bfloat16)
    d_gated = jnp.dot(grad, w_mamba_out.T, preferred_element_type=jnp.float32).astype(jnp.bfloat16)

    def core(a, b, c, d, e, f, h):
        return mixer_core(a, b, c, d, e, f, h, conv_inner, conv_state, step_bias, decay_rate, length)
    unused, pull = jax.vjp(core, query, key, value, inner, gate, state, raw_step)
    d_query, d_key, d_value, d_inner, d_gate, d_state, d_step = pull((d_attended, d_gated))
    d_normed = jnp.dot(d_query, w_query.T, preferred_element_type=jnp.float32)
    d_normed = d_normed + jnp.dot(d_key, w_key.T, preferred_element_type=jnp.float32)
    d_normed = d_normed + jnp.dot(d_value, w_value.T, preferred_element_type=jnp.float32)
    d_normed = d_normed + jnp.dot(d_inner, w_inner.T, preferred_element_type=jnp.float32)
    d_normed = d_normed + jnp.dot(d_gate, w_gate.T, preferred_element_type=jnp.float32)
    d_normed = d_normed + jnp.dot(d_state, w_state.astype(jnp.float32).T, precision=lax.Precision.HIGHEST)
    d_normed = d_normed + jnp.dot(d_step, w_step.astype(jnp.float32).T, precision=lax.Precision.HIGHEST)
    return (grad.astype(jnp.float32) + norm_back(x, gain, d_normed)).astype(jnp.bfloat16)

def reference(saved, cotangent, loss_grad, lengths, gain, w_query, w_key, w_value, w_attn_out, w_inner, w_gate, w_state, w_step, w_mamba_out, conv_inner, conv_state, step_bias, decay_rate):
    params = (gain, w_query, w_key, w_value, w_attn_out, w_inner, w_gate, w_state, w_step, w_mamba_out, conv_inner, conv_state, step_bias, decay_rate)

    def one_section(packed):
        return section_back(packed[0], packed[1], packed[2], packed[3:])
    first = lax.map(one_section, (saved[:, 0], cotangent, lengths[:, 0]) + params)
    upstream = jnp.concatenate([first[1:], loss_grad[None]], axis=0)
    return lax.map(one_section, (saved[:, 1], upstream, lengths[:, 1]) + params)
```

```python
import functools

import jax
import jax.numpy as jnp
from jax import lax
from jax.experimental import pallas as pl
from jax.experimental.pallas import tpu as pltpu
from jax.sharding import PartitionSpec as P

HEAD_SIZE = 128
MAMBA_HEAD = 64
STATE_SIZE = 128
TOKENS = 128
WIDTH = 2560
LANES = 128
F32 = jnp.float32
BF16 = jnp.bfloat16
HIGHEST = lax.Precision.HIGHEST

NN = (((1,), (0,)), ((), ()))
NT = (((1,), (1,)), ((), ()))
TN = (((0,), (0,)), ((), ()))

QUERY, KEY, VALUE, INNER, GATE, STATE = (
    (0, 256),
    (256, 128),
    (384, 128),
    (512, 512),
    (1024, 512),
    (1536, 256),
)
GROUPS = (QUERY, KEY, VALUE, INNER, GATE, STATE)
JOINED = 1792
ATTN_ROWS = 256
MAMBA_ROWS = 512
PAIRS = 4
HEADS = 8


def dot(a, b, dims=NN, precision=None):
    return lax.dot_general(a, b, dims, precision=precision, preferred_element_type=F32)


def dot_exact_left(a, b, dims):
    high = b.astype(BF16)
    low = (b - high.astype(F32)).astype(BF16)
    return dot(a, high, dims) + dot(a, low, dims)


def dot_exact_right(a, b, dims):
    high = a.astype(BF16)
    low = (a - high.astype(F32)).astype(BF16)
    rest = (a - high.astype(F32) - low.astype(F32)).astype(BF16)
    return dot(high, b, dims) + dot(low, b, dims) + dot(rest, b, dims)


def iota(shape, axis):
    return lax.broadcasted_iota(jnp.int32, shape, axis)


def conv_forward(values, taps):
    rows = iota(values.shape, 0)
    total = values * taps[3:4]
    for lag in (1, 2, 3):
        moved = jnp.where(rows >= lag, pltpu.roll(values, lag, 0), 0.0)
        total = total + moved * taps[3 - lag : 4 - lag]
    return total


def conv_backward(grads, taps):
    count = grads.shape[0]
    rows = iota(grads.shape, 0)
    total = grads * taps[3:4]
    for lag in (1, 2, 3):
        moved = jnp.where(rows < count - lag, pltpu.roll(grads, count - lag, 0), 0.0)
        total = total + moved * taps[3 - lag : 4 - lag]
    return total


def silu_parts(u):
    gate = jax.nn.sigmoid(u)
    value = u * gate
    return value, gate * (1.0 + u * (1.0 - gate))


def as_column(row):
    count = row.shape[1]
    square = jnp.broadcast_to(row, (count, count))
    eye = iota((count, count), 0) == iota((count, count), 1)
    return jnp.sum(jnp.where(eye, square, 0.0), axis=1, keepdims=True)


def low_lanes():
    return iota((TOKENS, LANES), 1) < MAMBA_HEAD


def tile_of(j):
    return slice(j * LANES, (j + 1) * LANES)


def forward(normed, ready, wcat, wstep, length, taps_inner, taps_state, bias, rate, save):
    def project(group):
        start, size = group
        ready(group)
        return dot(normed, wcat[:, start : start + size])

    query = project(QUERY).astype(BF16)
    key = project(KEY).astype(BF16)
    value = project(VALUE).astype(BF16)
    stacked = jnp.concatenate([query[:, :HEAD_SIZE], query[:, HEAD_SIZE:]], axis=0)
    save["query"][...] = stacked
    save["key"][...] = key
    save["value"][...] = value
    scores = dot(stacked, key, NT) * HEAD_SIZE ** (-0.5)
    row = iota(scores.shape, 0)
    row = jnp.where(row >= TOKENS, row - TOKENS, row)
    place = iota(scores.shape, 1)
    scores = jnp.where((place <= row) & (place < length), scores, -1e30)
    expo = jnp.exp(scores - jnp.max(scores, axis=-1, keepdims=True))
    save["probs"][...] = expo / jnp.sum(expo, axis=-1, keepdims=True)

    raw = dot(wstep, normed, NT) + as_column(bias)
    step = jnp.maximum(raw, 0.0) + jnp.log1p(jnp.exp(-jnp.abs(raw)))
    upper = (iota((TOKENS, TOKENS), 0) <= iota((TOKENS, TOKENS), 1)).astype(BF16)
    total = dot_exact_right(-step * as_column(rate), upper, NN)
    save["rows"][0:HEADS] = step
    save["rows"][HEADS : 2 * HEADS] = jax.nn.sigmoid(raw)
    padded = jnp.concatenate([total, step, jnp.zeros((TOKENS - 2 * HEADS, TOKENS), F32)], axis=0)
    columns = padded.T

    states, slope = silu_parts(conv_forward(project(STATE), taps_state))
    save["state_slope"][...] = slope
    b_in = states[:, :STATE_SIZE]
    c_out = states[:, STATE_SIZE:]
    save["states"][...] = states.astype(BF16)
    both = dot(c_out, b_in, NT, HIGHEST)

    inner = project(INNER).astype(BF16).astype(F32)
    mixed, slope = silu_parts(conv_forward(inner, taps_inner))
    save["mixed"][...] = mixed
    save["inner_slope"][...] = slope
    gate = project(GATE).astype(BF16).astype(F32)
    gated, slope = silu_parts(gate)
    save["gate"][...] = gated

    causal = iota((TOKENS, TOKENS), 1) <= iota((TOKENS, TOKENS), 0)
    low = low_lanes()
    for j in range(PAIRS):
        at = tile_of(j)
        stepped = [columns[:, HEADS + 2 * j + i : HEADS + 2 * j + i + 1] for i in (0, 1)]
        steps = jnp.where(
            low,
            jnp.broadcast_to(stepped[0], (TOKENS, LANES)),
            jnp.broadcast_to(stepped[1], (TOKENS, LANES)),
        )
        scaled = (mixed[:, at] * steps).astype(BF16)
        save["steps"][:, at] = steps
        save["scaled"][:, at] = scaled
        parts = []
        for h in (2 * j, 2 * j + 1):
            diffs = columns[:, h : h + 1] - total[h : h + 1, :]
            decay = jnp.exp(jnp.where(causal, diffs, -1e30))
            kernel = (both * decay).astype(BF16)
            save["decay"][:, h * LANES : (h + 1) * LANES] = decay
            save["kernel"][:, h * LANES : (h + 1) * LANES] = kernel
            parts.append(dot(kernel, scaled))
        summed = jnp.where(low, parts[0], parts[1])
        save["summed"][:, at] = summed
        save["gate_slope"][:, at] = (summed + mixed[:, at]) * slope[:, at]


def backward(grad, ready, wout, wcat, wstep, taps_inner, taps_state, rate, save, joined, out):
    ready("attn_out")
    d_attended = dot(grad, wout[:ATTN_ROWS, :], NT).astype(BF16)
    stacked = jnp.concatenate([d_attended[:, :HEAD_SIZE], d_attended[:, HEAD_SIZE:]], axis=0)
    probs = save["probs"][...]
    d_probs = dot(stacked, save["value"][...], NT).astype(BF16).astype(F32)
    weighted = probs * d_probs
    d_scores = weighted - probs * jnp.sum(weighted, axis=-1, keepdims=True)
    d_scores = (d_scores * HEAD_SIZE ** (-0.5)).astype(BF16)
    d_query = dot(d_scores, save["key"][...]).astype(BF16)
    joined[:, 0:HEAD_SIZE] = d_query[:TOKENS]
    joined[:, HEAD_SIZE : 2 * HEAD_SIZE] = d_query[TOKENS:]
    joined[:, 256:384] = dot(d_scores, save["query"][...], TN).astype(BF16)
    joined[:, 384:512] = dot(probs.astype(BF16), stacked, TN).astype(BF16)

    ready("mamba_out")
    d_gated = dot(grad, wout[ATTN_ROWS:, :], NT).astype(BF16).astype(F32)
    joined[:, 1024:1536] = (d_gated * save["gate_slope"][...]).astype(BF16)
    d_scan = d_gated * save["gate"][...]
    d_scan_low = d_scan.astype(BF16)
    low = low_lanes()
    d_both = jnp.zeros((TOKENS, TOKENS), F32)
    d_mixed = []
    decay_terms = []
    step_terms = []
    for j in range(PAIRS):
        at = tile_of(j)
        tile = d_scan_low[:, at]
        scaled = save["scaled"][:, at]
        parts = []
        for i in (0, 1):
            h = 2 * j + i
            heads = slice(h * LANES, (h + 1) * LANES)
            own = jnp.where(low if i == 0 else jnp.logical_not(low), tile, jnp.zeros_like(tile))
            d_both = d_both + dot(own, scaled, NT) * save["decay"][:, heads]
            parts.append(dot(save["kernel"][:, heads], tile, TN))
        pulled = jnp.where(low, parts[0], parts[1])
        d_mixed.append(save["steps"][:, at] * pulled + d_scan[:, at])
        decay_terms.append(d_scan[:, at] * save["summed"][:, at])
        step_terms.append(save["mixed"][:, at] * pulled)
    d_mixed = jnp.concatenate(d_mixed, axis=1)
    d_inner = conv_backward(d_mixed * save["inner_slope"][...], taps_inner)
    joined[:, 512:1024] = d_inner.astype(BF16)

    d_both = d_both.astype(BF16)
    d_b = dot(d_both, save["states"][:, STATE_SIZE:], TN)
    d_c = dot(d_both, save["states"][:, :STATE_SIZE])
    d_states = jnp.concatenate([d_b, d_c], axis=1) * save["state_slope"][...]
    joined[:, 1536:1792] = conv_backward(d_states, taps_state).astype(BF16)

    shape = (HEADS, MAMBA_ROWS)
    pick = (iota(shape, 1) // MAMBA_HEAD == iota(shape, 0)).astype(BF16)
    by_decay = dot_exact_left(pick, jnp.concatenate(decay_terms, axis=1), NT)
    by_step = dot_exact_left(pick, jnp.concatenate(step_terms, axis=1), NT)
    step = save["rows"][0:HEADS]
    d_total = by_decay - step * by_step
    lower = (iota((TOKENS, TOKENS), 0) >= iota((TOKENS, TOKENS), 1)).astype(BF16)
    d_log = dot_exact_right(d_total, lower, NN)
    d_raw = (by_step - as_column(rate) * d_log) * save["rows"][HEADS : 2 * HEADS]
    d_raw = d_raw.astype(BF16)

    for group in GROUPS:
        ready(group)
    size = 512
    for start in range(0, WIDTH, size):
        part = slice(start, start + size)
        total = dot(joined[...], wcat[part, :], NT) + dot(d_raw, wstep[:, part], TN)
        out[:, part] = total.astype(out.dtype)


SAVED = {
    "query": ((2 * TOKENS, HEAD_SIZE), BF16),
    "key": ((TOKENS, HEAD_SIZE), BF16),
    "value": ((TOKENS, HEAD_SIZE), BF16),
    "probs": ((2 * TOKENS, TOKENS), F32),
    "rows": ((2 * HEADS, TOKENS), F32),
    "states": ((TOKENS, 2 * STATE_SIZE), BF16),
    "state_slope": ((TOKENS, 2 * STATE_SIZE), F32),
    "mixed": ((TOKENS, MAMBA_ROWS), F32),
    "inner_slope": ((TOKENS, MAMBA_ROWS), F32),
    "gate": ((TOKENS, MAMBA_ROWS), F32),
    "gate_slope": ((TOKENS, MAMBA_ROWS), F32),
    "steps": ((TOKENS, MAMBA_ROWS), F32),
    "scaled": ((TOKENS, MAMBA_ROWS), BF16),
    "summed": ((TOKENS, MAMBA_ROWS), F32),
    "decay": ((TOKENS, HEADS * LANES), F32),
    "kernel": ((TOKENS, HEADS * LANES), BF16),
}
N_IN = len(GROUPS)


def start_copies(sources, wcat, wout, sems, names):
    copies = {}
    for name in names:
        if name == "attn_out":
            copy = pltpu.make_async_copy(sources[name], wout.at[:ATTN_ROWS, :], sems.at[N_IN])
        elif name == "mamba_out":
            copy = pltpu.make_async_copy(sources[name], wout.at[ATTN_ROWS:, :], sems.at[N_IN + 1])
        else:
            start, size = name
            copy = pltpu.make_async_copy(
                sources[name], wcat.at[:, start : start + size], sems.at[GROUPS.index(name)]
            )
        copy.start()
        copies[name] = copy
    waited = set()

    def ready(name):
        if name in copies and name not in waited:
            waited.add(name)
            copies[name].wait()

    return ready


def normalized(x_ref, gain_ref):
    x = x_ref[...].astype(F32)
    scale = lax.rsqrt(jnp.mean(x * x, axis=-1, keepdims=True) + 1e-05)
    return (x * scale * gain_ref[...]).astype(BF16)


def whole_kernel(which, length, x, grad, gain, wstep, taps_inner, taps_state, bias, rate, *refs):
    sources = dict(zip(GROUPS + ("attn_out", "mamba_out"), refs[: N_IN + 2]))
    out = refs[N_IN + 2]
    wcat, wout, joined, sems = refs[N_IN + 3 : N_IN + 7]
    save = dict(zip(SAVED, refs[N_IN + 7 :]))
    order = (QUERY, KEY, VALUE, STATE, INNER, GATE, "attn_out", "mamba_out")
    ready = start_copies(sources, wcat, wout, sems, order)
    taps_i = taps_inner[...].astype(F32)
    taps_s = taps_state[...].astype(F32)
    forward(
        normalized(x, gain),
        ready,
        wcat,
        wstep[...],
        length[0, which],
        taps_i,
        taps_s,
        bias[...],
        rate[...],
        save,
    )
    backward(
        grad[...], ready, wout, wcat, wstep, taps_i, taps_s, rate[...], save, joined, out
    )


def forward_kernel(which, length, x, gain, wstep, taps_inner, taps_state, bias, rate, *refs):
    sources = dict(zip(GROUPS, refs[:N_IN]))
    save = dict(zip(SAVED, refs[N_IN : N_IN + len(SAVED)]))
    wcat, sems = refs[N_IN + len(SAVED) :]
    order = (QUERY, KEY, VALUE, STATE, INNER, GATE)
    ready = start_copies(sources, wcat, None, sems, order)
    forward(
        normalized(x, gain),
        ready,
        wcat,
        wstep[...],
        length[0, which],
        taps_inner[...].astype(F32),
        taps_state[...].astype(F32),
        bias[...],
        rate[...],
        save,
    )


def backward_kernel(grad, wstep, taps_inner, taps_state, rate, *refs):
    sources = dict(zip(GROUPS + ("attn_out", "mamba_out"), refs[: N_IN + 2]))
    save = dict(zip(SAVED, refs[N_IN + 2 : N_IN + 2 + len(SAVED)]))
    out, wcat, wout, joined, sems = refs[N_IN + 2 + len(SAVED) :]
    order = ("attn_out", "mamba_out", QUERY, KEY, VALUE, STATE, INNER, GATE)
    ready = start_copies(sources, wcat, wout, sems, order)
    backward(
        grad[...],
        ready,
        wout,
        wcat,
        wstep,
        taps_inner[...].astype(F32),
        taps_state[...].astype(F32),
        rate[...],
        save,
        joined,
        out,
    )


VMEM = pl.BlockSpec(memory_space=pltpu.VMEM)
SMEM = pl.BlockSpec(memory_space=pltpu.SMEM)
ANY = pl.BlockSpec(memory_space=pl.ANY)
WCAT = pltpu.VMEM((WIDTH, JOINED), BF16)
WOUT = pltpu.VMEM((ATTN_ROWS + MAMBA_ROWS, WIDTH), BF16)
GRADS = pltpu.VMEM((TOKENS, JOINED), BF16)
SEMS = pltpu.SemaphoreType.DMA((N_IN + 2,))
PARAMS = pltpu.CompilerParams(vmem_limit_bytes=40 * 1024 * 1024)
PARTIAL = jax.ShapeDtypeStruct((TOKENS, WIDTH), BF16)


def whole_call(which, length, x, grad, small, weights):
    gain, wstep, taps_inner, taps_state, bias, rate = small
    return pl.pallas_call(
        functools.partial(whole_kernel, which),
        out_shape=PARTIAL,
        in_specs=[SMEM] + [VMEM] * 8 + [ANY] * (N_IN + 2),
        out_specs=VMEM,
        scratch_shapes=[WCAT, WOUT, GRADS, SEMS]
        + [pltpu.VMEM(shape, dtype) for shape, dtype in SAVED.values()],
        compiler_params=PARAMS,
        cost_estimate=pl.CostEstimate(
            flops=2 * TOKENS * WIDTH * 4352, bytes_accessed=16 << 20, transcendentals=1 << 19
        ),
        name="section",
    )(length, x, grad, gain, wstep, taps_inner, taps_state, bias, rate, *weights)


def forward_call(which, length, x, small, weights):
    gain, wstep, taps_inner, taps_state, bias, rate = small
    return pl.pallas_call(
        functools.partial(forward_kernel, which),
        out_shape=[jax.ShapeDtypeStruct(shape, dtype) for shape, dtype in SAVED.values()],
        in_specs=[SMEM] + [VMEM] * 7 + [ANY] * N_IN,
        out_specs=[VMEM] * len(SAVED),
        scratch_shapes=[WCAT, SEMS],
        compiler_params=PARAMS,
        cost_estimate=pl.CostEstimate(
            flops=2 * TOKENS * WIDTH * 1800, bytes_accessed=13 << 20, transcendentals=1 << 19
        ),
        name="second_forward",
    )(length, x, gain, wstep, taps_inner, taps_state, bias, rate, *weights[:N_IN])


def backward_call(grad, small, weights, saved):
    gain, wstep, taps_inner, taps_state, bias, rate = small
    return pl.pallas_call(
        backward_kernel,
        out_shape=PARTIAL,
        in_specs=[VMEM] * 5 + [ANY] * (N_IN + 2) + [VMEM] * len(SAVED),
        out_specs=VMEM,
        scratch_shapes=[WCAT, WOUT, GRADS, SEMS],
        compiler_params=PARAMS,
        cost_estimate=pl.CostEstimate(
            flops=2 * TOKENS * WIDTH * 2560, bytes_accessed=18 << 20, transcendentals=0
        ),
        name="second_backward",
    )(grad, wstep, taps_inner, taps_state, rate, *weights, *saved)


def finish_kernel(parts, x_ref, grad_ref, gain_ref, out):
    x = x_ref[...].astype(F32)
    scale = lax.rsqrt(jnp.mean(x * x, axis=-1, keepdims=True) + 1e-05)
    d_normed = jnp.sum(parts[...].astype(F32), axis=0)
    weighted = d_normed * gain_ref[...]
    mean = jnp.mean(x * weighted, axis=-1, keepdims=True)
    back = scale * weighted - x * (scale * scale * scale) * mean
    out[...] = (grad_ref[...].astype(F32) + back).astype(BF16)


def finish_call(parts, x, grad, gain):
    return pl.pallas_call(
        finish_kernel,
        out_shape=jax.ShapeDtypeStruct(x.shape, BF16),
        in_specs=[VMEM] * 4,
        out_specs=VMEM,
        compiler_params=PARAMS,
        name="finish",
    )(parts, x, grad, gain)


def exchange(blocks):
    return lax.all_to_all(blocks, "tensor", 0, 0)


def spread(rows):
    count = lax.axis_size("tensor")
    return exchange(jnp.broadcast_to(rows[None], (count,) + rows.shape))


def pass_back(values):
    count = lax.axis_size("pipe")
    return lax.ppermute(values, "pipe", [(i + 1, i) for i in range(count - 1)])


def per_device(
    saved,
    cotangent,
    loss_grad,
    lengths,
    gain,
    w_query,
    w_key,
    w_value,
    w_attn_out,
    w_inner,
    w_gate,
    w_state,
    w_step,
    w_mamba_out,
    conv_inner,
    conv_state,
    step_bias,
    decay_rate,
):
    small = (gain, w_step[0].T, conv_inner[0], conv_state[0], step_bias, decay_rate)
    weights = (
        w_query[0],
        w_key[0],
        w_value[0],
        w_inner[0],
        w_gate[0],
        w_state[0],
        w_attn_out[0],
        w_mamba_out[0],
    )
    count, rows = lax.axis_size("tensor"), loss_grad.shape[0]
    shape = (count * rows, WIDTH)
    gathered = spread(jnp.concatenate([saved[0, 0], cotangent[0], saved[0, 1]], axis=0))
    first_full = gathered[:, :rows].reshape(shape)
    grad_first = gathered[:, rows : 2 * rows].reshape(shape)
    second_full = gathered[:, 2 * rows :].reshape(shape)

    partial = whole_call(0, lengths, first_full, grad_first, small, weights)
    parts = exchange(partial.reshape(count, rows, WIDTH))
    first_back = finish_call(parts, saved[0, 0], cotangent[0], gain)
    received = pass_back(first_back)
    held = forward_call(1, lengths, second_full, small, weights)
    is_last = lax.axis_index("pipe") == lax.axis_size("pipe") - 1
    grad_rows = jnp.where(is_last, loss_grad, received)
    grad_second = spread(grad_rows).reshape(shape)
    partial = backward_call(grad_second, small, weights, held)
    parts = exchange(partial.reshape(count, rows, WIDTH))
    return finish_call(parts, saved[0, 1], grad_rows, gain)[None]


def solution(mesh):
    placed = (
        P("pipe", None, "tensor", None),
        P("pipe", "tensor", None),
        P("tensor", None),
        P("pipe", None),
        P("pipe", None),
        P("pipe", None, "tensor"),
        P("pipe", None, "tensor"),
        P("pipe", None, "tensor"),
        P("pipe", "tensor", None),
        P("pipe", None, "tensor"),
        P("pipe", None, "tensor"),
        P("pipe", None, None),
        P("pipe", None, "tensor"),
        P("pipe", "tensor", None),
        P("pipe", None, "tensor"),
        P("pipe", None, None),
        P("pipe", "tensor"),
        P("pipe", "tensor"),
    )
    return jax.shard_map(
        per_device, mesh=mesh, in_specs=placed, out_specs=P("pipe", "tensor", None), check_vma=False
    )
```

```python
import functools

import jax
import jax.numpy as jnp
from jax import lax
from jax.experimental import pallas as pl
from jax.experimental.pallas import tpu as pltpu
from jax.sharding import PartitionSpec as P

HEAD_SIZE = 128
MAMBA_HEAD = 64
STATE_SIZE = 128
TOKENS = 128
WIDTH = 2560
LANES = 128
F32 = jnp.float32
BF16 = jnp.bfloat16
HIGHEST = lax.Precision.HIGHEST

NN = (((1,), (0,)), ((), ()))
NT = (((1,), (1,)), ((), ()))
TN = (((0,), (0,)), ((), ()))

QUERY, KEY, VALUE, INNER, GATE, STATE = (
    (0, 256),
    (256, 128),
    (384, 128),
    (512, 512),
    (1024, 512),
    (1536, 256),
)
GROUPS = (QUERY, KEY, VALUE, INNER, GATE, STATE)
JOINED = 1792
PADDED = 1920
ATTN_ROWS = 256
MAMBA_ROWS = 512
PAIRS = 4
HEADS = 8


def dot(a, b, dims=NN, precision=None):
    return lax.dot_general(a, b, dims, precision=precision, preferred_element_type=F32)


def dot_exact_left(a, b, dims):
    high = b.astype(BF16)
    low = (b - high.astype(F32)).astype(BF16)
    return dot(a, high, dims) + dot(a, low, dims)


def dot_exact_right(a, b, dims):
    high = a.astype(BF16)
    low = (a - high.astype(F32)).astype(BF16)
    rest = (a - high.astype(F32) - low.astype(F32)).astype(BF16)
    return dot(high, b, dims) + dot(low, b, dims) + dot(rest, b, dims)


def iota(shape, axis):
    return lax.broadcasted_iota(jnp.int32, shape, axis)


def conv_forward(values, taps):
    rows = iota(values.shape, 0)
    total = values * taps[3:4]
    for lag in (1, 2, 3):
        moved = jnp.where(rows >= lag, pltpu.roll(values, lag, 0), 0.0)
        total = total + moved * taps[3 - lag : 4 - lag]
    return total


def conv_backward(grads, taps):
    count = grads.shape[0]
    rows = iota(grads.shape, 0)
    total = grads * taps[3:4]
    for lag in (1, 2, 3):
        moved = jnp.where(rows < count - lag, pltpu.roll(grads, count - lag, 0), 0.0)
        total = total + moved * taps[3 - lag : 4 - lag]
    return total


def silu_parts(u):
    gate = jax.nn.sigmoid(u)
    value = u * gate
    return value, gate * (1.0 + u * (1.0 - gate))


def as_column(row):
    count = row.shape[1]
    square = jnp.broadcast_to(row, (count, count))
    eye = iota((count, count), 0) == iota((count, count), 1)
    return jnp.sum(jnp.where(eye, square, 0.0), axis=1, keepdims=True)


def low_lanes():
    return iota((TOKENS, LANES), 1) < MAMBA_HEAD


def tile_of(j):
    return slice(j * LANES, (j + 1) * LANES)


def forward(normed, wcat, wstep, length, taps_inner, taps_state, bias, rate, save):
    def project(group):
        start, size = group
        return dot(normed, wcat[:, start : start + size])

    query = project(QUERY).astype(BF16)
    key = project(KEY).astype(BF16)
    value = project(VALUE).astype(BF16)
    stacked = jnp.concatenate([query[:, :HEAD_SIZE], query[:, HEAD_SIZE:]], axis=0)
    save["query"][...] = stacked
    save["key"][...] = key
    save["value"][...] = value
    scores = dot(stacked, key, NT) * HEAD_SIZE ** (-0.5)
    row = iota(scores.shape, 0)
    row = jnp.where(row >= TOKENS, row - TOKENS, row)
    place = iota(scores.shape, 1)
    scores = jnp.where((place <= row) & (place < length), scores, -1e30)
    expo = jnp.exp(scores - jnp.max(scores, axis=-1, keepdims=True))
    save["probs"][...] = expo / jnp.sum(expo, axis=-1, keepdims=True)

    raw = dot(wstep, normed, NT) + as_column(bias)
    step = jnp.maximum(raw, 0.0) + jnp.log1p(jnp.exp(-jnp.abs(raw)))
    upper = (iota((TOKENS, TOKENS), 0) <= iota((TOKENS, TOKENS), 1)).astype(BF16)
    total = dot_exact_right(-step * as_column(rate), upper, NN)
    save["rows"][0:HEADS] = step
    save["rows"][HEADS : 2 * HEADS] = jax.nn.sigmoid(raw)
    padded = jnp.concatenate([total, step, jnp.zeros((TOKENS - 2 * HEADS, TOKENS), F32)], axis=0)
    columns = padded.T

    states, slope = silu_parts(conv_forward(project(STATE), taps_state))
    save["state_slope"][...] = slope
    b_in = states[:, :STATE_SIZE]
    c_out = states[:, STATE_SIZE:]
    save["states"][...] = states.astype(BF16)
    both = dot(c_out, b_in, NT, HIGHEST)

    inner = project(INNER).astype(BF16).astype(F32)
    mixed, slope = silu_parts(conv_forward(inner, taps_inner))
    save["mixed"][...] = mixed
    save["inner_slope"][...] = slope
    gate = project(GATE).astype(BF16).astype(F32)
    gated, slope = silu_parts(gate)
    save["gate"][...] = gated

    causal = iota((TOKENS, TOKENS), 1) <= iota((TOKENS, TOKENS), 0)
    low = low_lanes()
    for j in range(PAIRS):
        at = tile_of(j)
        stepped = [columns[:, HEADS + 2 * j + i : HEADS + 2 * j + i + 1] for i in (0, 1)]
        steps = jnp.where(
            low,
            jnp.broadcast_to(stepped[0], (TOKENS, LANES)),
            jnp.broadcast_to(stepped[1], (TOKENS, LANES)),
        )
        scaled = (mixed[:, at] * steps).astype(BF16)
        save["steps"][:, at] = steps
        save["scaled"][:, at] = scaled
        parts = []
        for h in (2 * j, 2 * j + 1):
            diffs = columns[:, h : h + 1] - total[h : h + 1, :]
            decay = jnp.exp(jnp.where(causal, diffs, -1e30))
            kernel = (both * decay).astype(BF16)
            save["decay"][:, h * LANES : (h + 1) * LANES] = decay
            save["kernel"][:, h * LANES : (h + 1) * LANES] = kernel
            parts.append(dot(kernel, scaled))
        summed = jnp.where(low, parts[0], parts[1])
        save["summed"][:, at] = summed
        save["gate_slope"][:, at] = (summed + mixed[:, at]) * slope[:, at]


def backward(grad, wout, wback, taps_inner, taps_state, rate, save, joined, out):
    d_attended = dot(grad, wout[:, :ATTN_ROWS]).astype(BF16)
    stacked = jnp.concatenate([d_attended[:, :HEAD_SIZE], d_attended[:, HEAD_SIZE:]], axis=0)
    probs = save["probs"][...]
    d_probs = dot(stacked, save["value"][...], NT).astype(BF16).astype(F32)
    weighted = probs * d_probs
    d_scores = weighted - probs * jnp.sum(weighted, axis=-1, keepdims=True)
    d_scores = (d_scores * HEAD_SIZE ** (-0.5)).astype(BF16)
    d_query = dot(d_scores, save["key"][...]).astype(BF16)
    joined[:, 0:HEAD_SIZE] = d_query[:TOKENS]
    joined[:, HEAD_SIZE : 2 * HEAD_SIZE] = d_query[TOKENS:]
    joined[:, 256:384] = dot(d_scores, save["query"][...], TN).astype(BF16)
    joined[:, 384:512] = dot(probs.astype(BF16), stacked, TN).astype(BF16)

    d_gated = dot(grad, wout[:, ATTN_ROWS:]).astype(BF16).astype(F32)
    joined[:, 1024:1536] = (d_gated * save["gate_slope"][...]).astype(BF16)
    d_scan = d_gated * save["gate"][...]
    d_scan_low = d_scan.astype(BF16)
    low = low_lanes()
    d_both = jnp.zeros((TOKENS, TOKENS), F32)
    d_mixed = []
    decay_terms = []
    step_terms = []
    for j in range(PAIRS):
        at = tile_of(j)
        tile = d_scan_low[:, at]
        scaled = save["scaled"][:, at]
        parts = []
        for i in (0, 1):
            h = 2 * j + i
            heads = slice(h * LANES, (h + 1) * LANES)
            own = jnp.where(low if i == 0 else jnp.logical_not(low), tile, jnp.zeros_like(tile))
            d_both = d_both + dot(own, scaled, NT) * save["decay"][:, heads]
            parts.append(dot(save["kernel"][:, heads], tile, TN))
        pulled = jnp.where(low, parts[0], parts[1])
        d_mixed.append(save["steps"][:, at] * pulled + d_scan[:, at])
        decay_terms.append(d_scan[:, at] * save["summed"][:, at])
        step_terms.append(save["mixed"][:, at] * pulled)
    d_mixed = jnp.concatenate(d_mixed, axis=1)
    d_inner = conv_backward(d_mixed * save["inner_slope"][...], taps_inner)
    joined[:, 512:1024] = d_inner.astype(BF16)

    d_both = d_both.astype(BF16)
    d_b = dot(d_both, save["states"][:, STATE_SIZE:], TN)
    d_c = dot(d_both, save["states"][:, :STATE_SIZE])
    d_states = jnp.concatenate([d_b, d_c], axis=1) * save["state_slope"][...]
    joined[:, 1536:1792] = conv_backward(d_states, taps_state).astype(BF16)

    shape = (HEADS, MAMBA_ROWS)
    pick = (iota(shape, 1) // MAMBA_HEAD == iota(shape, 0)).astype(BF16)
    by_decay = dot_exact_left(pick, jnp.concatenate(decay_terms, axis=1), NT)
    by_step = dot_exact_left(pick, jnp.concatenate(step_terms, axis=1), NT)
    step = save["rows"][0:HEADS]
    d_total = by_decay - step * by_step
    lower = (iota((TOKENS, TOKENS), 0) >= iota((TOKENS, TOKENS), 1)).astype(BF16)
    d_log = dot_exact_right(d_total, lower, NN)
    d_raw = (by_step - as_column(rate) * d_log) * save["rows"][HEADS : 2 * HEADS]
    d_raw = jnp.concatenate([d_raw, jnp.zeros((TOKENS - HEADS, TOKENS), F32)], axis=0)
    joined[:, JOINED:] = d_raw.T.astype(BF16)

    size = WIDTH // len(WBACK)
    for part in WBACK:
        lanes = slice(part * size, (part + 1) * size)
        total = dot(joined[...], wback[part]).astype(out.dtype)
        out[:, : TOKENS // 8, lanes] = total.reshape(8, TOKENS // 8, size)


WBACK = (0, 1, 2, 3, 4)
SAVED = {
    "query": ((2 * TOKENS, HEAD_SIZE), BF16),
    "key": ((TOKENS, HEAD_SIZE), BF16),
    "value": ((TOKENS, HEAD_SIZE), BF16),
    "probs": ((2 * TOKENS, TOKENS), F32),
    "rows": ((2 * HEADS, TOKENS), F32),
    "states": ((TOKENS, 2 * STATE_SIZE), BF16),
    "state_slope": ((TOKENS, 2 * STATE_SIZE), F32),
    "mixed": ((TOKENS, MAMBA_ROWS), F32),
    "inner_slope": ((TOKENS, MAMBA_ROWS), F32),
    "gate": ((TOKENS, MAMBA_ROWS), F32),
    "gate_slope": ((TOKENS, MAMBA_ROWS), F32),
    "steps": ((TOKENS, MAMBA_ROWS), F32),
    "scaled": ((TOKENS, MAMBA_ROWS), BF16),
    "summed": ((TOKENS, MAMBA_ROWS), F32),
    "decay": ((TOKENS, HEADS * LANES), F32),
    "kernel": ((TOKENS, HEADS * LANES), BF16),
}
N_IN = len(GROUPS)


def row_scale(x):
    return lax.rsqrt(jnp.mean(x * x, axis=-1, keepdims=True) + 1e-05)


def normalized(x_ref, gain_ref):
    x = x_ref[...].reshape(TOKENS, WIDTH).astype(F32)
    return (x * row_scale(x) * gain_ref[...]).astype(BF16)


def turn_kernel(wstep_from, *refs):
    sources = refs[: N_IN + 2]
    wcat, turned, wback, wout, wstep, sems = refs[N_IN + 2 :]
    load_step = pltpu.make_async_copy(wstep_from, wstep, sems.at[N_IN + 2])
    load_step.start()
    loads = []
    for i, (start, size) in enumerate(GROUPS):
        target = wcat.at[:, start : start + size]
        loads.append(pltpu.make_async_copy(sources[i], target, sems.at[i]))
    for i, rows in enumerate((slice(0, ATTN_ROWS), slice(ATTN_ROWS, ATTN_ROWS + MAMBA_ROWS))):
        loads.append(pltpu.make_async_copy(sources[N_IN + i], wout.at[rows], sems.at[N_IN + i]))
    for load in loads:
        load.start()
    size = WIDTH // len(WBACK)
    wback[:, JOINED:, :] = jnp.zeros((len(WBACK), PADDED - JOINED, size), BF16)
    load_step.wait()
    for part in WBACK:
        wback[part, JOINED : JOINED + 16, :] = jnp.concatenate(
            [wstep[:, part * size : (part + 1) * size], jnp.zeros((8, size), BF16)], axis=0
        )
    for load, (start, columns) in zip(loads, GROUPS):
        load.wait()
        for part in WBACK:
            block = wcat[part * size : (part + 1) * size, start : start + columns]
            wback[part, start : start + columns, :] = block.T
    for load in loads[N_IN:]:
        load.wait()
    for start in range(0, ATTN_ROWS + MAMBA_ROWS, 256):
        turned[:, start : start + 256] = wout[start : start + 256, :].T


def place(me, blocks, lanes_of):
    for step in range(4):
        owner = lax.rem(me + 8 - 2 * step, 8)
        pair = owner + 1 - 2 * lax.rem(owner, 2)
        for index, target in lanes_of:
            target[owner] = blocks[step][index]
            target[pair] = blocks[4 + step][index]


def whole_kernel(info, lengths, saved, *refs):
    blocks, refs = refs[:8], refs[8:]
    gain, wstep, taps_inner, taps_state, bias, rate, wcat, wout, wback, out = refs[:10]
    x, grad, joined = refs[10:13]
    save = dict(zip(SAVED, refs[13:]))
    place(lax.rem(info[0], 8), blocks, ((0, x), (1, grad)))
    rows = x.shape[1]
    for i in range(8):
        out[i, rows:] = saved[0, 1]
    taps_i = taps_inner[...].astype(F32)
    taps_s = taps_state[...].astype(F32)
    forward(
        normalized(x, gain),
        wcat,
        wstep[...],
        lengths[0, 0],
        taps_i,
        taps_s,
        bias[...],
        rate[...],
        save,
    )
    backward(
        grad[...].reshape(TOKENS, WIDTH),
        wout,
        wback,
        taps_i,
        taps_s,
        rate[...],
        save,
        joined,
        out,
    )


def forward_kernel(lengths, x, *refs):
    gain, wstep, taps_inner, taps_state, bias, rate, wcat = refs[:7]
    save = dict(zip(SAVED, refs[7:]))
    forward(
        normalized(x.at[:, TOKENS // 8 :], gain),
        wcat,
        wstep[...],
        lengths[0, 1],
        taps_inner[...].astype(F32),
        taps_state[...].astype(F32),
        bias[...],
        rate[...],
        save,
    )


def backward_kernel(info, *refs):
    blocks, refs = refs[:4], refs[4:]
    taps_inner, taps_state, rate, wout, wback = refs[:5]
    save = dict(zip(SAVED, refs[5 : 5 + len(SAVED)]))
    out, grad, joined = refs[5 + len(SAVED) :]
    halves = [block.at[i : i + 1] for i in (0, 1) for block in blocks]
    place(lax.rem(info[0], 8), halves, ((0, grad),))
    backward(
        grad[...].reshape(TOKENS, WIDTH),
        wout,
        wback,
        taps_inner[...].astype(F32),
        taps_state[...].astype(F32),
        rate[...],
        save,
        joined,
        out,
    )


VMEM = pl.BlockSpec(memory_space=pltpu.VMEM)
SMEM = pl.BlockSpec(memory_space=pltpu.SMEM)
HBM = pl.BlockSpec(memory_space=pltpu.HBM)
WCAT_SHAPE = (WIDTH, JOINED)
WOUT_SHAPE = (WIDTH, ATTN_ROWS + MAMBA_ROWS)
WBACK_SHAPE = (len(WBACK), PADDED, WIDTH // len(WBACK))
GRADS = pltpu.VMEM((TOKENS, PADDED), BF16)
HELD = [pltpu.VMEM(shape, dtype) for shape, dtype in SAVED.values()]
ROWS = pltpu.VMEM((8, TOKENS // 8, WIDTH), BF16)
PARAMS = pltpu.CompilerParams(vmem_limit_bytes=16 * 1024 * 1024)


def in_hbm(arrays):
    return [pltpu.with_memory_space_constraint(array, pltpu.HBM) for array in arrays]


def in_vmem(arrays):
    return [pltpu.with_memory_space_constraint(array, pltpu.VMEM) for array in arrays]


def turn_call(wstep, weights):
    return pl.pallas_call(
        turn_kernel,
        out_shape=[pltpu.VMEM(s, BF16) for s in (WCAT_SHAPE, WOUT_SHAPE, WBACK_SHAPE)],
        in_specs=[HBM] * (N_IN + 3),
        out_specs=[VMEM] * 3,
        scratch_shapes=[
            pltpu.VMEM((ATTN_ROWS + MAMBA_ROWS, WIDTH), BF16),
            pltpu.VMEM((HEADS, WIDTH), BF16),
            pltpu.SemaphoreType.DMA((N_IN + 3,)),
        ],
        compiler_params=PARAMS,
        cost_estimate=pl.CostEstimate(flops=0, bytes_accessed=26 << 20, transcendentals=0),
        name="turn_weights",
    )(*in_hbm([wstep]), *in_hbm(weights))


def whole_call(info, lengths, saved, blocks, small, turned):
    return pl.pallas_call(
        whole_kernel,
        out_shape=jax.ShapeDtypeStruct((8, TOKENS // 4, WIDTH), BF16),
        in_specs=[SMEM] * 2 + [VMEM] * 18,
        out_specs=VMEM,
        scratch_shapes=[ROWS, ROWS, GRADS] + HELD,
        compiler_params=PARAMS,
        cost_estimate=pl.CostEstimate(
            flops=2 * TOKENS * WIDTH * 4352, bytes_accessed=24 << 20, transcendentals=1 << 19
        ),
        name="section",
    )(info, lengths, saved, *blocks, *small, *in_vmem(turned))


def forward_call(lengths, parts, small, turned):
    return pl.pallas_call(
        forward_kernel,
        out_shape=[pltpu.VMEM(shape, dtype) for shape, dtype in SAVED.values()],
        in_specs=[SMEM] + [VMEM] * 8,
        out_specs=[VMEM] * len(SAVED),
        compiler_params=PARAMS,
        cost_estimate=pl.CostEstimate(
            flops=2 * TOKENS * WIDTH * 1800, bytes_accessed=13 << 20, transcendentals=1 << 19
        ),
        name="second_forward",
    )(lengths, parts, *small, *in_vmem(turned[:1]))


def backward_call(info, blocks, small, turned, saved):
    gain, wstep, taps_inner, taps_state, bias, rate = small
    return pl.pallas_call(
        backward_kernel,
        out_shape=jax.ShapeDtypeStruct((8, TOKENS // 8, WIDTH), BF16),
        in_specs=[SMEM] + [VMEM] * (9 + len(SAVED)),
        out_specs=VMEM,
        scratch_shapes=[ROWS, GRADS],
        compiler_params=PARAMS,
        cost_estimate=pl.CostEstimate(
            flops=2 * TOKENS * WIDTH * 2560, bytes_accessed=18 << 20, transcendentals=0
        ),
        name="second_backward",
    )(
        info, *blocks, taps_inner, taps_state, rate, *in_vmem(turned[1:]), *in_vmem(saved)
    )


def pack_kernel(saved, cotangent, out, sems):
    copies = [
        pltpu.make_async_copy(saved.at[0, 0:1], out.at[0:1], sems.at[0]),
        pltpu.make_async_copy(cotangent, out.at[1:2], sems.at[1]),
    ]
    for copy in copies:
        copy.start()
    for copy in copies:
        copy.wait()


def pack_call(saved, cotangent):
    return pl.pallas_call(
        pack_kernel,
        out_shape=jax.ShapeDtypeStruct((2,) + cotangent.shape[1:], BF16),
        in_specs=[HBM] * 2,
        out_specs=VMEM,
        scratch_shapes=[pltpu.SemaphoreType.DMA((2,))],
        compiler_params=PARAMS,
        name="pack",
    )(*in_hbm([saved, cotangent]))


def pair_kernel(own, other, out):
    out[0] = own[...]
    out[1] = other[...]


def pair_call(own, other):
    return pl.pallas_call(
        pair_kernel,
        out_shape=jax.ShapeDtypeStruct((2,) + own.shape, BF16),
        in_specs=[VMEM] * 2,
        out_specs=VMEM,
        compiler_params=PARAMS,
        name="pair",
    )(own, other)


def finish_kernel(which, info, parts, saved, grad_ref, gain_ref, other, out):
    x = saved[0, which].astype(F32)
    scale = row_scale(x)
    d_normed = jnp.sum(parts[:, : x.shape[0]].astype(F32), axis=0)
    weighted = d_normed * gain_ref[...]
    mean = jnp.mean(x * weighted, axis=-1, keepdims=True)
    back = scale * weighted - x * (scale * scale * scale) * mean
    out[...] = (grad_ref[...].reshape(x.shape).astype(F32) + back).astype(BF16)
    if which == 0:

        @pl.when(info[0] >= 8)
        def _():
            out[...] = other[...]


def finish_call(which, info, parts, saved, grad, gain, other):
    return pl.pallas_call(
        functools.partial(finish_kernel, which),
        out_shape=jax.ShapeDtypeStruct(other.shape, BF16),
        in_specs=[SMEM] + [VMEM] * 5,
        out_specs=VMEM,
        compiler_params=PARAMS,
        name="finish",
    )(info, parts, saved, grad, gain, other)


def exchange(blocks):
    return lax.all_to_all(blocks, "tensor", 0, 0)


def to_pair(values):
    count = lax.axis_size("tensor")
    return lax.ppermute(values, "tensor", [(i, i ^ 1) for i in range(count)])


def around(block):
    count = lax.axis_size("tensor")
    moved = {
        step: lax.ppermute(block, "tensor", [(i, (i + 2 * step) % count) for i in range(count)])
        for step in (1, 3, 2)
    }
    return [block, moved[1], moved[2], moved[3]]


def pass_back(values, flip):
    sections, count = lax.axis_size("pipe"), lax.axis_size("tensor")
    route = [
        ((i + 1) % sections * count + j, i * count + (j ^ flip))
        for i in range(sections)
        for j in range(count)
    ]
    return lax.ppermute(values, ("pipe", "tensor"), route)


def per_device(
    saved,
    cotangent,
    loss_grad,
    lengths,
    gain,
    w_query,
    w_key,
    w_value,
    w_attn_out,
    w_inner,
    w_gate,
    w_state,
    w_step,
    w_mamba_out,
    conv_inner,
    conv_state,
    step_bias,
    decay_rate,
):
    small = (gain, w_step[0].T, conv_inner[0], conv_state[0], step_bias, decay_rate)
    weights = (
        w_query[0],
        w_key[0],
        w_value[0],
        w_inner[0],
        w_gate[0],
        w_state[0],
        w_attn_out[0],
        w_mamba_out[0],
    )
    is_first = (lax.axis_index("pipe") == 0).astype(jnp.int32)
    info = (lax.axis_index("tensor").astype(jnp.int32) + 8 * is_first).reshape(1)

    own = pack_call(saved, cotangent)
    other = to_pair(own)
    blocks = around(own) + around(other)
    query, other = lax.optimization_barrier((weights[0], other))
    turned = turn_call(small[1], (query,) + weights[1:])
    parts = exchange(whole_call(info, lengths, saved, blocks, small, turned))
    first_back = finish_call(0, info, parts, saved, cotangent, gain, loss_grad)
    own, other = pass_back(first_back, 0), pass_back(first_back, 1)
    parts, first_back = lax.optimization_barrier((parts, first_back))
    held = forward_call(lengths, parts, small, turned)
    grad_blocks = around(pair_call(own, other))
    parts = exchange(backward_call(info, grad_blocks, small, turned, held))
    return finish_call(1, info, parts, saved, own, gain, loss_grad)[None]


def solution(mesh):
    placed = (
        P("pipe", None, "tensor", None),
        P("pipe", "tensor", None),
        P("tensor", None),
        P("pipe", None),
        P("pipe", None),
        P("pipe", None, "tensor"),
        P("pipe", None, "tensor"),
        P("pipe", None, "tensor"),
        P("pipe", "tensor", None),
        P("pipe", None, "tensor"),
        P("pipe", None, "tensor"),
        P("pipe", None, None),
        P("pipe", None, "tensor"),
        P("pipe", "tensor", None),
        P("pipe", None, "tensor"),
        P("pipe", None, None),
        P("pipe", "tensor"),
        P("pipe", "tensor"),
    )
    return jax.shard_map(
        per_device, mesh=mesh, in_specs=placed, out_specs=P("pipe", "tensor", None), check_vma=False
    )
```

```python
import functools

import jax
import jax.numpy as jnp
from jax import lax
from jax.experimental import pallas as pl
from jax.experimental.pallas import tpu as pltpu
from jax.sharding import PartitionSpec as P

HEAD_SIZE = 128
MAMBA_HEAD = 64
STATE_SIZE = 128
TOKENS = 128
WIDTH = 2560
LANES = 128
F32 = jnp.float32
BF16 = jnp.bfloat16
HIGHEST = lax.Precision.HIGHEST

NN = (((1,), (0,)), ((), ()))
NT = (((1,), (1,)), ((), ()))
TN = (((0,), (0,)), ((), ()))

QUERY, KEY, VALUE, INNER, GATE, STATE = (
    (0, 256),
    (256, 128),
    (384, 128),
    (512, 512),
    (1024, 512),
    (1536, 256),
)
GROUPS = (QUERY, KEY, VALUE, INNER, GATE, STATE)
JOINED = 1792
PADDED = 1920
ATTN_ROWS = 256
MAMBA_ROWS = 512
PAIRS = 4
HEADS = 8


def dot(a, b, dims=NN, precision=None):
    return lax.dot_general(a, b, dims, precision=precision, preferred_element_type=F32)


def dot_split(a, b, exact, pieces):
    rest = b if exact == 0 else a
    total = 0.0
    for _ in range(pieces):
        part = rest.astype(BF16)
        rest = rest - part.astype(F32)
        total = total + (dot(a, part) if exact == 0 else dot(part, b))
    return total


def iota(shape, axis):
    return lax.broadcasted_iota(jnp.int32, shape, axis)


def conv_forward(values, taps):
    rows = iota(values.shape, 0)
    total = values * taps[3:4]
    for lag in (1, 2, 3):
        moved = jnp.where(rows >= lag, pltpu.roll(values, lag, 0), 0.0)
        total = total + moved * taps[3 - lag : 4 - lag]
    return total


def conv_backward(grads, taps):
    count = grads.shape[0]
    rows = iota(grads.shape, 0)
    total = grads * taps[3:4]
    for lag in (1, 2, 3):
        moved = jnp.where(rows < count - lag, pltpu.roll(grads, count - lag, 0), 0.0)
        total = total + moved * taps[3 - lag : 4 - lag]
    return total


def silu_parts(u):
    gate = jax.nn.sigmoid(u)
    value = u * gate
    return value, gate * (1.0 + u * (1.0 - gate))


def widened(row):
    return jnp.concatenate([row, jnp.zeros((1, LANES - row.shape[1]), F32)], axis=1)


def low_lanes():
    return iota((TOKENS, LANES), 1) < MAMBA_HEAD


def tile_of(j):
    return slice(j * LANES, (j + 1) * LANES)


def forward(normed, wcat, length, taps_inner, taps_state, bias, rate, save):
    def project(group, more=0):
        start, size = group[0], group[1] + more
        return dot(normed, wcat[:, start : start + size])

    query = project(QUERY).astype(BF16)
    key = project(KEY).astype(BF16)
    value = project(VALUE).astype(BF16)
    stacked = jnp.concatenate([query[:, :HEAD_SIZE], query[:, HEAD_SIZE:]], axis=0)
    save["query"][...] = stacked
    save["key"][...] = key
    save["value"][...] = value
    scores = dot(stacked, key, NT) * HEAD_SIZE ** (-0.5)
    row = iota(scores.shape, 0)
    row = jnp.where(row >= TOKENS, row - TOKENS, row)
    place = iota(scores.shape, 1)
    scores = jnp.where((place <= row) & (place < length), scores, -1e30)
    expo = jnp.exp(scores - jnp.max(scores, axis=-1, keepdims=True))
    save["probs"][...] = expo / jnp.sum(expo, axis=-1, keepdims=True)

    projected = project(STATE, LANES)
    raw = projected[:, 2 * STATE_SIZE :] + widened(bias)
    step = jnp.maximum(raw, 0.0) + jnp.log1p(jnp.exp(-jnp.abs(raw)))
    earlier = iota((TOKENS, TOKENS), 1) <= iota((TOKENS, TOKENS), 0)
    total = dot_split(earlier.astype(BF16), -step * widened(rate), 0, 3)
    save["step"][...] = step
    save["step_slope"][...] = jax.nn.sigmoid(raw)
    total_rows = total.T

    states, slope = silu_parts(conv_forward(projected[:, : 2 * STATE_SIZE], taps_state))
    save["state_slope"][...] = slope
    b_in = states[:, :STATE_SIZE]
    c_out = states[:, STATE_SIZE:]
    save["states"][...] = states.astype(BF16)
    both = dot(c_out, b_in, NT, HIGHEST)

    inner = project(INNER).astype(BF16).astype(F32)
    mixed, slope = silu_parts(conv_forward(inner, taps_inner))
    save["mixed"][...] = mixed
    save["inner_slope"][...] = slope
    gate = project(GATE).astype(BF16).astype(F32)
    gated, slope = silu_parts(gate)
    save["gate"][...] = gated

    low = low_lanes()
    for j in range(PAIRS):
        at = tile_of(j)
        stepped = [step[:, h : h + 1] for h in (2 * j, 2 * j + 1)]
        steps = jnp.where(
            low,
            jnp.broadcast_to(stepped[0], (TOKENS, LANES)),
            jnp.broadcast_to(stepped[1], (TOKENS, LANES)),
        )
        scaled = (mixed[:, at] * steps).astype(BF16)
        save["steps"][:, at] = steps
        save["scaled"][:, at] = scaled
        parts = []
        for h in (2 * j, 2 * j + 1):
            diffs = total[:, h : h + 1] - total_rows[h : h + 1, :]
            decay = jnp.exp(jnp.where(earlier, diffs, -1e30))
            kernel = (both * decay).astype(BF16)
            save["decay"][:, h * LANES : (h + 1) * LANES] = decay
            save["kernel"][:, h * LANES : (h + 1) * LANES] = kernel
            parts.append(dot(kernel, scaled))
        summed = jnp.where(low, parts[0], parts[1])
        save["summed"][:, at] = summed
        save["gate_slope"][:, at] = (summed + mixed[:, at]) * slope[:, at]


def backward(grad, wout, wback, taps_inner, taps_state, rate, save, joined, out):
    d_attended = dot(grad, wout[:, :ATTN_ROWS]).astype(BF16)
    stacked = jnp.concatenate([d_attended[:, :HEAD_SIZE], d_attended[:, HEAD_SIZE:]], axis=0)
    probs = save["probs"][...]
    d_probs = dot(stacked, save["value"][...], NT).astype(BF16).astype(F32)
    weighted = probs * d_probs
    d_scores = weighted - probs * jnp.sum(weighted, axis=-1, keepdims=True)
    d_scores = (d_scores * HEAD_SIZE ** (-0.5)).astype(BF16)
    d_query = dot(d_scores, save["key"][...]).astype(BF16)
    joined[:, 0:HEAD_SIZE] = d_query[:TOKENS]
    joined[:, HEAD_SIZE : 2 * HEAD_SIZE] = d_query[TOKENS:]
    joined[:, 256:384] = dot(d_scores, save["query"][...], TN).astype(BF16)
    joined[:, 384:512] = dot(probs.astype(BF16), stacked, TN).astype(BF16)

    d_gated = dot(grad, wout[:, ATTN_ROWS:]).astype(BF16).astype(F32)
    joined[:, 1024:1536] = (d_gated * save["gate_slope"][...]).astype(BF16)
    d_scan = d_gated * save["gate"][...]
    d_scan_low = d_scan.astype(BF16)
    low = low_lanes()
    d_both = jnp.zeros((TOKENS, TOKENS), F32)
    d_mixed = []
    decay_terms = []
    step_terms = []
    for j in range(PAIRS):
        at = tile_of(j)
        tile = d_scan_low[:, at]
        scaled = save["scaled"][:, at]
        parts = []
        for i in (0, 1):
            h = 2 * j + i
            heads = slice(h * LANES, (h + 1) * LANES)
            own = jnp.where(low if i == 0 else jnp.logical_not(low), tile, jnp.zeros_like(tile))
            d_both = d_both + dot(own, scaled, NT) * save["decay"][:, heads]
            parts.append(dot(save["kernel"][:, heads], tile, TN))
        pulled = jnp.where(low, parts[0], parts[1])
        d_mixed.append(save["steps"][:, at] * pulled + d_scan[:, at])
        decay_terms.append(d_scan[:, at] * save["summed"][:, at])
        step_terms.append(save["mixed"][:, at] * pulled)
    d_mixed = jnp.concatenate(d_mixed, axis=1)
    d_inner = conv_backward(d_mixed * save["inner_slope"][...], taps_inner)
    joined[:, 512:1024] = d_inner.astype(BF16)

    d_both = d_both.astype(BF16)
    d_b = dot(d_both, save["states"][:, STATE_SIZE:], TN)
    d_c = dot(d_both, save["states"][:, :STATE_SIZE])
    d_states = jnp.concatenate([d_b, d_c], axis=1) * save["state_slope"][...]
    joined[:, 1536:1792] = conv_backward(d_states, taps_state).astype(BF16)

    shape = (MAMBA_ROWS, LANES)
    pick = (iota(shape, 0) // MAMBA_HEAD == iota(shape, 1)).astype(BF16)
    by_decay = dot_split(jnp.concatenate(decay_terms, axis=1), pick, 1, 2)
    by_step = dot_split(jnp.concatenate(step_terms, axis=1), pick, 1, 2)
    d_total = by_decay - save["step"][...] * by_step
    later = iota((TOKENS, TOKENS), 1) >= iota((TOKENS, TOKENS), 0)
    d_log = dot_split(later.astype(BF16), d_total, 0, 3)
    d_raw = (by_step - widened(rate) * d_log) * save["step_slope"][...]
    joined[:, JOINED:] = d_raw.astype(BF16)

    size = WIDTH // len(WBACK)
    for part in WBACK:
        lanes = slice(part * size, (part + 1) * size)
        total = dot(joined[...], wback[part]).astype(out.dtype)
        out[:, : TOKENS // 8, lanes] = total.reshape(8, TOKENS // 8, size)


WBACK = (0, 1, 2, 3, 4)
SAVED = {
    "query": ((2 * TOKENS, HEAD_SIZE), BF16),
    "key": ((TOKENS, HEAD_SIZE), BF16),
    "value": ((TOKENS, HEAD_SIZE), BF16),
    "probs": ((2 * TOKENS, TOKENS), F32),
    "step": ((TOKENS, LANES), F32),
    "step_slope": ((TOKENS, LANES), F32),
    "states": ((TOKENS, 2 * STATE_SIZE), BF16),
    "state_slope": ((TOKENS, 2 * STATE_SIZE), F32),
    "mixed": ((TOKENS, MAMBA_ROWS), F32),
    "inner_slope": ((TOKENS, MAMBA_ROWS), F32),
    "gate": ((TOKENS, MAMBA_ROWS), F32),
    "gate_slope": ((TOKENS, MAMBA_ROWS), F32),
    "steps": ((TOKENS, MAMBA_ROWS), F32),
    "scaled": ((TOKENS, MAMBA_ROWS), BF16),
    "summed": ((TOKENS, MAMBA_ROWS), F32),
    "decay": ((TOKENS, HEADS * LANES), F32),
    "kernel": ((TOKENS, HEADS * LANES), BF16),
}
N_IN = len(GROUPS)


def row_scale(x):
    return lax.rsqrt(jnp.mean(x * x, axis=-1, keepdims=True) + 1e-05)


def normalized(x_ref, gain_ref):
    x = x_ref[...].reshape(TOKENS, WIDTH).astype(F32)
    return (x * row_scale(x) * gain_ref[...]).astype(BF16)


def turn_kernel(wstep_from, *refs):
    sources = refs[: N_IN + 2]
    wcat, turned, wback, wout, wstep, sems = refs[N_IN + 2 :]
    load_step = pltpu.make_async_copy(wstep_from, wstep, sems.at[N_IN + 2])
    load_step.start()
    loads = []
    for i, (start, size) in enumerate(GROUPS):
        target = wcat.at[:, start : start + size]
        loads.append(pltpu.make_async_copy(sources[i], target, sems.at[i]))
    for i, rows in enumerate((slice(0, ATTN_ROWS), slice(ATTN_ROWS, ATTN_ROWS + MAMBA_ROWS))):
        loads.append(pltpu.make_async_copy(sources[N_IN + i], wout.at[rows], sems.at[N_IN + i]))
    for load in loads:
        load.start()
    size = WIDTH // len(WBACK)
    wback[:, JOINED:, :] = jnp.zeros((len(WBACK), PADDED - JOINED, size), BF16)
    load_step.wait()
    for part in WBACK:
        wback[part, JOINED : JOINED + 16, :] = jnp.concatenate(
            [wstep[:, part * size : (part + 1) * size], jnp.zeros((8, size), BF16)], axis=0
        )
        block = wback[part, JOINED:, :]
        wcat[part * size : (part + 1) * size, JOINED:] = block.T
    for load, (start, columns) in zip(loads, GROUPS):
        load.wait()
        for part in WBACK:
            block = wcat[part * size : (part + 1) * size, start : start + columns]
            wback[part, start : start + columns, :] = block.T
    for load in loads[N_IN:]:
        load.wait()
    for start in range(0, ATTN_ROWS + MAMBA_ROWS, 256):
        turned[:, start : start + 256] = wout[start : start + 256, :].T


def place(me, blocks, lanes_of):
    for step in range(4):
        owner = lax.rem(me + 8 - 2 * step, 8)
        pair = owner + 1 - 2 * lax.rem(owner, 2)
        for index, target in lanes_of:
            target[owner] = blocks[step][index]
            target[pair] = blocks[4 + step][index]


def whole_kernel(info, lengths, *refs):
    blocks, refs = refs[:8], refs[8:]
    second, second_other, gain, taps_inner, taps_state, bias, rate = refs[:7]
    wcat, wout, wback = refs[7:10]
    outs, joined_second = refs[10:14], refs[14]
    x, grad, total, joined = refs[15:19]
    save = dict(zip(SAVED, refs[19:]))
    me = lax.rem(info[0], 8)
    place(me, blocks, ((0, x), (1, grad)))
    joined_second[0] = second[0]
    joined_second[1] = second_other[0]
    taps_i = taps_inner[...].astype(F32)
    taps_s = taps_state[...].astype(F32)
    forward(
        normalized(x, gain),
        wcat,
        lengths[0, 0],
        taps_i,
        taps_s,
        bias[...],
        rate[...],
        save,
    )
    backward(
        grad[...].reshape(TOKENS, WIDTH),
        wout,
        wback,
        taps_i,
        taps_s,
        rate[...],
        save,
        joined,
        total,
    )
    for step, out in enumerate(outs):
        owner = lax.rem(me + 2 * step, 8)
        out[0] = total[owner]
        out[1] = total[owner + 1 - 2 * lax.rem(owner, 2)]


def forward_kernel(info, lengths, *refs):
    blocks, refs = refs[:4], refs[4:]
    gain, taps_inner, taps_state, bias, rate, wcat = refs[:6]
    save = dict(zip(SAVED, refs[6 : 6 + len(SAVED)]))
    x = refs[6 + len(SAVED)]
    halves = [block.at[i : i + 1] for i in (0, 1) for block in blocks]
    place(lax.rem(info[0], 8), halves, ((0, x),))
    forward(
        normalized(x, gain),
        wcat,
        lengths[0, 1],
        taps_inner[...].astype(F32),
        taps_state[...].astype(F32),
        bias[...],
        rate[...],
        save,
    )


def backward_kernel(info, *refs):
    blocks, refs = refs[:4], refs[4:]
    taps_inner, taps_state, rate, wout, wback = refs[:5]
    save = dict(zip(SAVED, refs[5 : 5 + len(SAVED)]))
    out, grad, joined = refs[5 + len(SAVED) :]
    halves = [block.at[i : i + 1] for i in (0, 1) for block in blocks]
    place(lax.rem(info[0], 8), halves, ((0, grad),))
    backward(
        grad[...].reshape(TOKENS, WIDTH),
        wout,
        wback,
        taps_inner[...].astype(F32),
        taps_state[...].astype(F32),
        rate[...],
        save,
        joined,
        out,
    )


VMEM = pl.BlockSpec(memory_space=pltpu.VMEM)
SMEM = pl.BlockSpec(memory_space=pltpu.SMEM)
HBM = pl.BlockSpec(memory_space=pltpu.HBM)
WCAT_SHAPE = (WIDTH, PADDED)
WOUT_SHAPE = (WIDTH, ATTN_ROWS + MAMBA_ROWS)
WBACK_SHAPE = (len(WBACK), PADDED, WIDTH // len(WBACK))
GRADS = pltpu.VMEM((TOKENS, PADDED), BF16)
HELD = [pltpu.VMEM(shape, dtype) for shape, dtype in SAVED.values()]
ROWS = pltpu.VMEM((8, TOKENS // 8, WIDTH), BF16)
PARAMS = pltpu.CompilerParams(vmem_limit_bytes=16 * 1024 * 1024)


def in_hbm(arrays):
    return [pltpu.with_memory_space_constraint(array, pltpu.HBM) for array in arrays]


def in_vmem(arrays):
    return [pltpu.with_memory_space_constraint(array, pltpu.VMEM) for array in arrays]


def turn_call(wstep, weights):
    return pl.pallas_call(
        turn_kernel,
        out_shape=[pltpu.VMEM(s, BF16) for s in (WCAT_SHAPE, WOUT_SHAPE, WBACK_SHAPE)],
        in_specs=[HBM] * (N_IN + 3),
        out_specs=[VMEM] * 3,
        scratch_shapes=[
            pltpu.VMEM((ATTN_ROWS + MAMBA_ROWS, WIDTH), BF16),
            pltpu.VMEM((HEADS, WIDTH), BF16),
            pltpu.SemaphoreType.DMA((N_IN + 3,)),
        ],
        compiler_params=PARAMS,
        cost_estimate=pl.CostEstimate(flops=0, bytes_accessed=26 << 20, transcendentals=0),
        name="turn_weights",
    )(*in_hbm([wstep]), *in_hbm(weights))


PAIR = (2, TOKENS // 8, WIDTH)


def whole_call(info, lengths, blocks, seconds, small, turned):
    return pl.pallas_call(
        whole_kernel,
        out_shape=[jax.ShapeDtypeStruct(PAIR, BF16)] * 5,
        in_specs=[SMEM] * 2 + [VMEM] * 18,
        out_specs=[VMEM] * 5,
        scratch_shapes=[ROWS, ROWS, ROWS, GRADS] + HELD,
        compiler_params=PARAMS,
        cost_estimate=pl.CostEstimate(
            flops=2 * TOKENS * WIDTH * 4352, bytes_accessed=24 << 20, transcendentals=1 << 19
        ),
        name="section",
    )(info, lengths, *blocks, *seconds, *small, *in_vmem(turned))


def forward_call(info, lengths, blocks, small, turned):
    return pl.pallas_call(
        forward_kernel,
        out_shape=[pltpu.VMEM(shape, dtype) for shape, dtype in SAVED.values()],
        in_specs=[SMEM] * 2 + [VMEM] * 10,
        out_specs=[VMEM] * len(SAVED),
        scratch_shapes=[ROWS],
        compiler_params=PARAMS,
        cost_estimate=pl.CostEstimate(
            flops=2 * TOKENS * WIDTH * 1800, bytes_accessed=13 << 20, transcendentals=1 << 19
        ),
        name="second_forward",
    )(info, lengths, *blocks, *small, *in_vmem(turned[:1]))


def backward_call(info, blocks, small, turned, saved):
    gain, taps_inner, taps_state, bias, rate = small
    return pl.pallas_call(
        backward_kernel,
        out_shape=jax.ShapeDtypeStruct((8, TOKENS // 8, WIDTH), BF16),
        in_specs=[SMEM] + [VMEM] * (9 + len(SAVED)),
        out_specs=VMEM,
        scratch_shapes=[ROWS, GRADS],
        compiler_params=PARAMS,
        cost_estimate=pl.CostEstimate(
            flops=2 * TOKENS * WIDTH * 2560, bytes_accessed=18 << 20, transcendentals=0
        ),
        name="second_backward",
    )(
        info, *blocks, taps_inner, taps_state, rate, *in_vmem(turned[1:]), *in_vmem(saved)
    )


def pack_kernel(saved, cotangent, first, second, sems):
    copies = [
        pltpu.make_async_copy(saved.at[0, 0:1], first.at[0:1], sems.at[0]),
        pltpu.make_async_copy(cotangent, first.at[1:2], sems.at[1]),
        pltpu.make_async_copy(saved.at[0, 1:2], second, sems.at[2]),
    ]
    for copy in copies:
        copy.start()
    for copy in copies:
        copy.wait()


def pack_call(saved, cotangent):
    rows = cotangent.shape[1:]
    return pl.pallas_call(
        pack_kernel,
        out_shape=[jax.ShapeDtypeStruct((n,) + rows, BF16) for n in (2, 1)],
        in_specs=[HBM] * 2,
        out_specs=[VMEM] * 2,
        scratch_shapes=[pltpu.SemaphoreType.DMA((3,))],
        compiler_params=PARAMS,
        name="pack",
    )(*in_hbm([saved, cotangent]))


def merge_kernel(info, *refs):
    parts, (own, other, gain, loss, out) = refs[:4], refs[4:]
    for i, block in enumerate((own, other)):
        x = block[0].astype(F32)
        scale = row_scale(x)
        d_normed = sum(part[i].astype(F32) for part in parts)
        weighted = d_normed * gain[...]
        mean = jnp.mean(x * weighted, axis=-1, keepdims=True)
        back = scale * weighted - x * (scale * scale * scale) * mean
        if i == 0:
            back = back + own[1].astype(F32)
        out[i] = back.astype(BF16)

    @pl.when((info[0] >= 8) & (info[0] < 16))
    def _():
        out[0] = loss[...]


def merge_call(info, parts, own, other, gain, loss):
    return pl.pallas_call(
        merge_kernel,
        out_shape=jax.ShapeDtypeStruct(PAIR, BF16),
        in_specs=[SMEM] + [VMEM] * 8,
        out_specs=VMEM,
        compiler_params=PARAMS,
        name="merge",
    )(info, *parts, own, other, gain, loss)


def pair_kernel(info, own, other, loss, out, rows):
    total = (own[0].astype(F32) + other[1].astype(F32)).astype(BF16)
    out[0] = total
    rows[...] = total
    out[1] = (own[1].astype(F32) + other[0].astype(F32)).astype(BF16)

    @pl.when(info[0] >= 16)
    def _():
        out[0] = loss[...]
        rows[...] = loss[...]
        out[1] = other[0]


def pair_call(info, own, other, loss):
    return pl.pallas_call(
        pair_kernel,
        out_shape=[jax.ShapeDtypeStruct(shape, BF16) for shape in (PAIR, PAIR[1:])],
        in_specs=[SMEM] + [VMEM] * 3,
        out_specs=[VMEM] * 2,
        compiler_params=PARAMS,
        name="pair",
    )(info, own, other, loss)


def finish_kernel(parts, saved, grad_ref, gain_ref, out):
    x = saved[0, 1].astype(F32)
    scale = row_scale(x)
    d_normed = jnp.sum(parts[...].astype(F32), axis=0)
    weighted = d_normed * gain_ref[...]
    mean = jnp.mean(x * weighted, axis=-1, keepdims=True)
    back = scale * weighted - x * (scale * scale * scale) * mean
    out[...] = (grad_ref[...].astype(F32) + back).astype(BF16)


def finish_call(parts, saved, grad, gain):
    return pl.pallas_call(
        finish_kernel,
        out_shape=jax.ShapeDtypeStruct(grad.shape, BF16),
        in_specs=[VMEM] * 4,
        out_specs=VMEM,
        compiler_params=PARAMS,
        name="finish",
    )(parts, saved, grad, gain)


def exchange(blocks):
    return lax.all_to_all(blocks, "tensor", 0, 0)


def to_pair(values):
    count = lax.axis_size("tensor")
    return lax.ppermute(values, "tensor", [(i, i ^ 1) for i in range(count)])


def step_ahead(block, step):
    count = lax.axis_size("tensor")
    return lax.ppermute(block, "tensor", [(i, (i + 2 * step) % count) for i in range(count)])


def around(block):
    moved = {step: step_ahead(block, step) for step in (1, 3, 2)}
    return [block, moved[1], moved[2], moved[3]]


def pass_back(values, flip):
    sections, count = lax.axis_size("pipe"), lax.axis_size("tensor")
    route = [
        ((i + 1) % sections * count + j, i * count + (j ^ (1 if i == sections - 1 else flip)))
        for i in range(sections)
        for j in range(count)
    ]
    return lax.ppermute(values, ("pipe", "tensor"), route)


def per_device(
    saved,
    cotangent,
    loss_grad,
    lengths,
    gain,
    w_query,
    w_key,
    w_value,
    w_attn_out,
    w_inner,
    w_gate,
    w_state,
    w_step,
    w_mamba_out,
    conv_inner,
    conv_state,
    step_bias,
    decay_rate,
):
    wstep = w_step[0].T
    small = (gain, conv_inner[0], conv_state[0], step_bias, decay_rate)
    weights = (
        w_query[0],
        w_key[0],
        w_value[0],
        w_inner[0],
        w_gate[0],
        w_state[0],
        w_attn_out[0],
        w_mamba_out[0],
    )
    place = lax.axis_index("pipe")
    is_first = (place == 0).astype(jnp.int32)
    is_last = (place == lax.axis_size("pipe") - 1).astype(jnp.int32)
    info = lax.axis_index("tensor").astype(jnp.int32) + 8 * is_first + 16 * is_last
    info = info.reshape(1)

    own, second = pack_call(saved, cotangent)
    other = to_pair(own)
    blocks = around(own) + around(other)
    query, second, other = lax.optimization_barrier((weights[0], second, other))
    turned = turn_call(wstep, (query,) + weights[1:])
    seconds = (second, to_pair(second))
    *parts, second = whole_call(info, lengths, blocks, seconds, small, turned)
    parts = [parts[0]] + [step_ahead(parts[step], step) for step in (1, 3, 2)]
    onward, backward = step_ahead(second, 1), step_ahead(second, 3)
    parts, onward, backward = lax.optimization_barrier((parts, onward, backward))
    second_blocks = [second, onward, step_ahead(backward, 3), backward]
    merged = merge_call(info, parts, own, other, gain, loss_grad)
    own, other = pass_back(merged, 0), pass_back(merged, 1)
    second_blocks, merged = lax.optimization_barrier((second_blocks, merged))
    held = forward_call(info, lengths, second_blocks, small, turned)
    grad_block, grad_rows = pair_call(info, own, other, loss_grad)
    grad_blocks = around(grad_block)
    parts = exchange(backward_call(info, grad_blocks, small, turned, held))
    return finish_call(parts, saved, grad_rows, gain)[None]


def solution(mesh):
    placed = (
        P("pipe", None, "tensor", None),
        P("pipe", "tensor", None),
        P("tensor", None),
        P("pipe", None),
        P("pipe", None),
        P("pipe", None, "tensor"),
        P("pipe", None, "tensor"),
        P("pipe", None, "tensor"),
        P("pipe", "tensor", None),
        P("pipe", None, "tensor"),
        P("pipe", None, "tensor"),
        P("pipe", None, None),
        P("pipe", None, "tensor"),
        P("pipe", "tensor", None),
        P("pipe", None, "tensor"),
        P("pipe", None, None),
        P("pipe", "tensor"),
        P("pipe", "tensor"),
    )
    return jax.shard_map(
        per_device, mesh=mesh, in_specs=placed, out_specs=P("pipe", "tensor", None), check_vma=False
    )
```

```python
import functools

import jax
import jax.numpy as jnp
from jax import lax
from jax.experimental import pallas as pl
from jax.experimental.pallas import tpu as pltpu
from jax.sharding import PartitionSpec as P

HEAD_SIZE = 128
MAMBA_HEAD = 64
STATE_SIZE = 128
TOKENS = 128
WIDTH = 2560
LANES = 128
F32 = jnp.float32
BF16 = jnp.bfloat16
HIGHEST = lax.Precision.HIGHEST

NN = (((1,), (0,)), ((), ()))
NT = (((1,), (1,)), ((), ()))
TN = (((0,), (0,)), ((), ()))

QUERY, KEY, VALUE, INNER, GATE, STATE = (
    (0, 256),
    (256, 128),
    (384, 128),
    (512, 512),
    (1024, 512),
    (1536, 256),
)
GROUPS = (QUERY, KEY, VALUE, INNER, GATE, STATE)
JOINED = 1792
PADDED = 1920
ATTN_ROWS = 256
MAMBA_ROWS = 512
PAIRS = 4
HEADS = 8


def dot(a, b, dims=NN, precision=None):
    return lax.dot_general(a, b, dims, precision=precision, preferred_element_type=F32)


def dot_split(a, b, exact, pieces):
    rest = b if exact == 0 else a
    total = 0.0
    for _ in range(pieces):
        part = rest.astype(BF16)
        rest = rest - part.astype(F32)
        total = total + (dot(a, part) if exact == 0 else dot(part, b))
    return total


def iota(shape, axis):
    return lax.broadcasted_iota(jnp.int32, shape, axis)


def conv_forward(values, taps):
    rows = iota(values.shape, 0)
    total = values * taps[3:4]
    for lag in (1, 2, 3):
        moved = jnp.where(rows >= lag, pltpu.roll(values, lag, 0), 0.0)
        total = total + moved * taps[3 - lag : 4 - lag]
    return total


def conv_backward(grads, taps):
    count = grads.shape[0]
    rows = iota(grads.shape, 0)
    total = grads * taps[3:4]
    for lag in (1, 2, 3):
        moved = jnp.where(rows < count - lag, pltpu.roll(grads, count - lag, 0), 0.0)
        total = total + moved * taps[3 - lag : 4 - lag]
    return total


def silu_parts(u):
    gate = jax.nn.sigmoid(u)
    value = u * gate
    return value, gate * (1.0 + u * (1.0 - gate))


def widened(row):
    return jnp.concatenate([row, jnp.zeros((1, LANES - row.shape[1]), F32)], axis=1)


def low_lanes():
    return iota((TOKENS, LANES), 1) < MAMBA_HEAD


def tile_of(j):
    return slice(j * LANES, (j + 1) * LANES)


def forward(normed, wcat, length, taps_inner, taps_state, bias, rate, save):
    def project(group, more=0):
        start, size = group[0], group[1] + more
        return dot(normed, wcat[:, start : start + size])

    query = project(QUERY).astype(BF16)
    key = project(KEY).astype(BF16)
    value = project(VALUE).astype(BF16)
    stacked = jnp.concatenate([query[:, :HEAD_SIZE], query[:, HEAD_SIZE:]], axis=0)
    save["query"][...] = stacked
    save["key"][...] = key
    save["value"][...] = value
    scores = dot(stacked, key, NT) * HEAD_SIZE ** (-0.5)
    row = iota(scores.shape, 0)
    row = jnp.where(row >= TOKENS, row - TOKENS, row)
    place = iota(scores.shape, 1)
    scores = jnp.where((place <= row) & (place < length), scores, -1e30)
    expo = jnp.exp(scores - jnp.max(scores, axis=-1, keepdims=True))
    save["probs"][...] = expo / jnp.sum(expo, axis=-1, keepdims=True)

    projected = project(STATE, LANES)
    raw = projected[:, 2 * STATE_SIZE :] + widened(bias)
    step = jnp.maximum(raw, 0.0) + jnp.log1p(jnp.exp(-jnp.abs(raw)))
    earlier = iota((TOKENS, TOKENS), 1) <= iota((TOKENS, TOKENS), 0)
    total = dot_split(earlier.astype(BF16), -step * widened(rate), 0, 3)
    save["step"][...] = step
    save["step_slope"][...] = jax.nn.sigmoid(raw)
    total_rows = total.T

    states, slope = silu_parts(conv_forward(projected[:, : 2 * STATE_SIZE], taps_state))
    save["state_slope"][...] = slope
    b_in = states[:, :STATE_SIZE]
    c_out = states[:, STATE_SIZE:]
    save["states"][...] = states.astype(BF16)
    both = dot(c_out, b_in, NT, HIGHEST)

    inner = project(INNER).astype(BF16).astype(F32)
    mixed, slope = silu_parts(conv_forward(inner, taps_inner))
    save["mixed"][...] = mixed
    save["inner_slope"][...] = slope
    gate = project(GATE).astype(BF16).astype(F32)
    gated, slope = silu_parts(gate)
    save["gate"][...] = gated

    low = low_lanes()
    for j in range(PAIRS):
        at = tile_of(j)
        stepped = [step[:, h : h + 1] for h in (2 * j, 2 * j + 1)]
        steps = jnp.where(
            low,
            jnp.broadcast_to(stepped[0], (TOKENS, LANES)),
            jnp.broadcast_to(stepped[1], (TOKENS, LANES)),
        )
        scaled = (mixed[:, at] * steps).astype(BF16)
        save["steps"][:, at] = steps
        save["scaled"][:, at] = scaled
        parts = []
        for h in (2 * j, 2 * j + 1):
            diffs = total[:, h : h + 1] - total_rows[h : h + 1, :]
            decay = jnp.exp(jnp.where(earlier, diffs, -1e30))
            kernel = (both * decay).astype(BF16)
            save["decay"][:, h * LANES : (h + 1) * LANES] = decay
            save["kernel"][:, h * LANES : (h + 1) * LANES] = kernel
            parts.append(dot(kernel, scaled))
        summed = jnp.where(low, parts[0], parts[1])
        save["summed"][:, at] = summed
        save["gate_slope"][:, at] = (summed + mixed[:, at]) * slope[:, at]


def backward(grad, wout, wback, taps_inner, taps_state, rate, save, joined, out):
    d_attended = dot(grad, wout[:, :ATTN_ROWS]).astype(BF16)
    stacked = jnp.concatenate([d_attended[:, :HEAD_SIZE], d_attended[:, HEAD_SIZE:]], axis=0)
    probs = save["probs"][...]
    d_probs = dot(stacked, save["value"][...], NT).astype(BF16).astype(F32)
    weighted = probs * d_probs
    d_scores = weighted - probs * jnp.sum(weighted, axis=-1, keepdims=True)
    d_scores = (d_scores * HEAD_SIZE ** (-0.5)).astype(BF16)
    d_query = dot(d_scores, save["key"][...]).astype(BF16)
    joined[:, 0:HEAD_SIZE] = d_query[:TOKENS]
    joined[:, HEAD_SIZE : 2 * HEAD_SIZE] = d_query[TOKENS:]
    joined[:, 256:384] = dot(d_scores, save["query"][...], TN).astype(BF16)
    joined[:, 384:512] = dot(probs.astype(BF16), stacked, TN).astype(BF16)

    d_gated = dot(grad, wout[:, ATTN_ROWS:]).astype(BF16).astype(F32)
    joined[:, 1024:1536] = (d_gated * save["gate_slope"][...]).astype(BF16)
    d_scan = d_gated * save["gate"][...]
    d_scan_low = d_scan.astype(BF16)
    low = low_lanes()
    d_both = jnp.zeros((TOKENS, TOKENS), F32)
    d_mixed = []
    decay_terms = []
    step_terms = []
    for j in range(PAIRS):
        at = tile_of(j)
        tile = d_scan_low[:, at]
        scaled = save["scaled"][:, at]
        parts = []
        for i in (0, 1):
            h = 2 * j + i
            heads = slice(h * LANES, (h + 1) * LANES)
            own = jnp.where(low if i == 0 else jnp.logical_not(low), tile, jnp.zeros_like(tile))
            d_both = d_both + dot(own, scaled, NT) * save["decay"][:, heads]
            parts.append(dot(save["kernel"][:, heads], tile, TN))
        pulled = jnp.where(low, parts[0], parts[1])
        d_mixed.append(save["steps"][:, at] * pulled + d_scan[:, at])
        decay_terms.append(d_scan[:, at] * save["summed"][:, at])
        step_terms.append(save["mixed"][:, at] * pulled)
    d_mixed = jnp.concatenate(d_mixed, axis=1)
    d_inner = conv_backward(d_mixed * save["inner_slope"][...], taps_inner)
    joined[:, 512:1024] = d_inner.astype(BF16)

    d_both = d_both.astype(BF16)
    d_b = dot(d_both, save["states"][:, STATE_SIZE:], TN)
    d_c = dot(d_both, save["states"][:, :STATE_SIZE])
    d_states = jnp.concatenate([d_b, d_c], axis=1) * save["state_slope"][...]
    joined[:, 1536:1792] = conv_backward(d_states, taps_state).astype(BF16)

    shape = (MAMBA_ROWS, LANES)
    pick = (iota(shape, 0) // MAMBA_HEAD == iota(shape, 1)).astype(BF16)
    by_decay = dot_split(jnp.concatenate(decay_terms, axis=1), pick, 1, 2)
    by_step = dot_split(jnp.concatenate(step_terms, axis=1), pick, 1, 2)
    d_total = by_decay - save["step"][...] * by_step
    later = iota((TOKENS, TOKENS), 1) >= iota((TOKENS, TOKENS), 0)
    d_log = dot_split(later.astype(BF16), d_total, 0, 3)
    d_raw = (by_step - widened(rate) * d_log) * save["step_slope"][...]
    joined[:, JOINED:] = d_raw.astype(BF16)

    size = WIDTH // len(WBACK)
    for part in WBACK:
        lanes = slice(part * size, (part + 1) * size)
        total = dot(joined[...], wback[part]).astype(out.dtype)
        out[:, : TOKENS // 8, lanes] = total.reshape(8, TOKENS // 8, size)


WBACK = (0, 1, 2, 3, 4)
SAVED = {
    "query": ((2 * TOKENS, HEAD_SIZE), BF16),
    "key": ((TOKENS, HEAD_SIZE), BF16),
    "value": ((TOKENS, HEAD_SIZE), BF16),
    "probs": ((2 * TOKENS, TOKENS), F32),
    "step": ((TOKENS, LANES), F32),
    "step_slope": ((TOKENS, LANES), F32),
    "states": ((TOKENS, 2 * STATE_SIZE), BF16),
    "state_slope": ((TOKENS, 2 * STATE_SIZE), F32),
    "mixed": ((TOKENS, MAMBA_ROWS), F32),
    "inner_slope": ((TOKENS, MAMBA_ROWS), F32),
    "gate": ((TOKENS, MAMBA_ROWS), F32),
    "gate_slope": ((TOKENS, MAMBA_ROWS), F32),
    "steps": ((TOKENS, MAMBA_ROWS), F32),
    "scaled": ((TOKENS, MAMBA_ROWS), BF16),
    "summed": ((TOKENS, MAMBA_ROWS), F32),
    "decay": ((TOKENS, HEADS * LANES), F32),
    "kernel": ((TOKENS, HEADS * LANES), BF16),
}
N_IN = len(GROUPS)


def row_scale(x):
    return lax.rsqrt(jnp.mean(x * x, axis=-1, keepdims=True) + 1e-05)


def normalized(x_ref, gain_ref):
    x = x_ref[...].reshape(TOKENS, WIDTH).astype(F32)
    return (x * row_scale(x) * gain_ref[...]).astype(BF16)


def turn_kernel(wstep_from, *refs):
    sources = refs[: N_IN + 2]
    wcat, turned, wback, wout, wstep, sems = refs[N_IN + 2 :]
    load_step = pltpu.make_async_copy(wstep_from, wstep, sems.at[N_IN + 3])
    load_step.start()
    size = WIDTH // len(WBACK)
    loads = []
    for i, (start, columns) in enumerate(GROUPS):
        target = wcat.at[:, start : start + columns]
        loads.append(pltpu.make_async_copy(sources[i], target, sems.at[i]))
    for i, (source, start) in enumerate(((N_IN, 0), (N_IN + 1, 0), (N_IN + 1, 256))):
        rows = slice(256 * i, 256 * (i + 1))
        piece = sources[source].at[start : start + 256]
        loads.append(pltpu.make_async_copy(piece, wout.at[rows], sems.at[N_IN + i]))
    order = (3, 4, 7, 8, 6, 0, 5, 1, 2)
    for i in order:
        loads[i].start()
    wback[:, JOINED:, :] = jnp.zeros((len(WBACK), PADDED - JOINED, size), BF16)
    load_step.wait()
    for part in WBACK:
        wback[part, JOINED : JOINED + 16, :] = jnp.concatenate(
            [wstep[:, part * size : (part + 1) * size], jnp.zeros((8, size), BF16)], axis=0
        )
        block = wback[part, JOINED:, :]
        wcat[part * size : (part + 1) * size, JOINED:] = block.T
    for i in order:
        loads[i].wait()
        if i < N_IN:
            start, columns = GROUPS[i]
            for part in WBACK:
                block = wcat[part * size : (part + 1) * size, start : start + columns]
                wback[part, start : start + columns, :] = block.T
        else:
            rows = slice(256 * (i - N_IN), 256 * (i - N_IN + 1))
            turned[:, rows] = wout[rows, :].T


def place(me, blocks, lanes_of):
    for step in range(4):
        owner = lax.rem(me + 8 - 2 * step, 8)
        pair = owner + 1 - 2 * lax.rem(owner, 2)
        for index, target in lanes_of:
            target[owner] = blocks[step][index]
            target[pair] = blocks[4 + step][index]


def whole_kernel(info, lengths, *refs):
    blocks, refs = refs[:8], refs[8:]
    gain, taps_inner, taps_state, bias, rate = refs[:5]
    wcat, wout, wback = refs[5:8]
    outs = refs[8:12]
    x, grad, total, joined = refs[12:16]
    save = dict(zip(SAVED, refs[16:]))
    me = lax.rem(info[0], 8)
    place(me, blocks, ((0, x), (1, grad)))
    taps_i = taps_inner[...].astype(F32)
    taps_s = taps_state[...].astype(F32)
    forward(
        normalized(x, gain),
        wcat,
        lengths[0, 0],
        taps_i,
        taps_s,
        bias[...],
        rate[...],
        save,
    )
    backward(
        grad[...].reshape(TOKENS, WIDTH),
        wout,
        wback,
        taps_i,
        taps_s,
        rate[...],
        save,
        joined,
        total,
    )
    for step, out in enumerate(outs):
        owner = lax.rem(me + 2 * step, 8)
        out[0] = total[owner]
        out[1] = total[owner + 1 - 2 * lax.rem(owner, 2)]


def forward_kernel(info, lengths, *refs):
    own, other, refs = refs[0], refs[1], refs[2:]
    gain, taps_inner, taps_state, bias, rate, wcat = refs[:6]
    save = dict(zip(SAVED, refs[6 : 6 + len(SAVED)]))
    x = refs[6 + len(SAVED)]
    quarters = [block.at[i : i + 1] for block in (own, other) for i in range(4)]
    place(lax.rem(info[0], 8), quarters, ((0, x),))
    forward(
        normalized(x, gain),
        wcat,
        lengths[0, 1],
        taps_inner[...].astype(F32),
        taps_state[...].astype(F32),
        bias[...],
        rate[...],
        save,
    )


def backward_kernel(info, *refs):
    (block, next_one, last_one, far, far_pair), refs = refs[:5], refs[5:]
    taps_inner, taps_state, rate, wout, wback = refs[:5]
    save = dict(zip(SAVED, refs[5 : 5 + len(SAVED)]))
    out, grad, joined = refs[5 + len(SAVED) :]
    halves = [
        own
        for i, apart in enumerate((far, far_pair))
        for own in (block.at[i : i + 1], next_one.at[i : i + 1], apart, last_one.at[i : i + 1])
    ]
    place(lax.rem(info[0], 8), halves, ((0, grad),))
    backward(
        grad[...].reshape(TOKENS, WIDTH),
        wout,
        wback,
        taps_inner[...].astype(F32),
        taps_state[...].astype(F32),
        rate[...],
        save,
        joined,
        out,
    )


VMEM = pl.BlockSpec(memory_space=pltpu.VMEM)
SMEM = pl.BlockSpec(memory_space=pltpu.SMEM)
HBM = pl.BlockSpec(memory_space=pltpu.HBM)
WCAT_SHAPE = (WIDTH, PADDED)
WOUT_SHAPE = (WIDTH, ATTN_ROWS + MAMBA_ROWS)
WBACK_SHAPE = (len(WBACK), PADDED, WIDTH // len(WBACK))
GRADS = pltpu.VMEM((TOKENS, PADDED), BF16)
HELD = [pltpu.VMEM(shape, dtype) for shape, dtype in SAVED.values()]
ROWS = pltpu.VMEM((8, TOKENS // 8, WIDTH), BF16)
PARAMS = pltpu.CompilerParams(vmem_limit_bytes=16 * 1024 * 1024)


def in_hbm(arrays):
    return [pltpu.with_memory_space_constraint(array, pltpu.HBM) for array in arrays]


def in_vmem(arrays):
    return [pltpu.with_memory_space_constraint(array, pltpu.VMEM) for array in arrays]


def turn_call(wstep, weights):
    return pl.pallas_call(
        turn_kernel,
        out_shape=[pltpu.VMEM(s, BF16) for s in (WCAT_SHAPE, WOUT_SHAPE, WBACK_SHAPE)],
        in_specs=[HBM] * (N_IN + 3),
        out_specs=[VMEM] * 3,
        scratch_shapes=[
            pltpu.VMEM((ATTN_ROWS + MAMBA_ROWS, WIDTH), BF16),
            pltpu.VMEM((HEADS, WIDTH), BF16),
            pltpu.SemaphoreType.DMA((N_IN + 4,)),
        ],
        compiler_params=PARAMS,
        cost_estimate=pl.CostEstimate(flops=0, bytes_accessed=26 << 20, transcendentals=0),
        name="turn_weights",
    )(*in_hbm([wstep]), *in_hbm(weights))


PAIR = (2, TOKENS // 8, WIDTH)


def whole_call(info, lengths, blocks, small, turned):
    return pl.pallas_call(
        whole_kernel,
        out_shape=[jax.ShapeDtypeStruct(PAIR, BF16)] * 4,
        in_specs=[SMEM] * 2 + [VMEM] * 16,
        out_specs=[VMEM] * 4,
        scratch_shapes=[ROWS, ROWS, ROWS, GRADS] + HELD,
        compiler_params=PARAMS,
        cost_estimate=pl.CostEstimate(
            flops=2 * TOKENS * WIDTH * 4352, bytes_accessed=24 << 20, transcendentals=1 << 19
        ),
        name="section",
    )(info, lengths, *blocks, *small, *in_vmem(turned))


def forward_call(info, lengths, blocks, small, turned):
    return pl.pallas_call(
        forward_kernel,
        out_shape=[pltpu.VMEM(shape, dtype) for shape, dtype in SAVED.values()],
        in_specs=[SMEM] * 2 + [VMEM] * 8,
        out_specs=[VMEM] * len(SAVED),
        scratch_shapes=[ROWS],
        compiler_params=PARAMS,
        cost_estimate=pl.CostEstimate(
            flops=2 * TOKENS * WIDTH * 1800, bytes_accessed=13 << 20, transcendentals=1 << 19
        ),
        name="second_forward",
    )(info, lengths, *blocks, *small, *in_vmem(turned[:1]))


def backward_call(info, blocks, small, turned, saved):
    gain, taps_inner, taps_state, bias, rate = small
    return pl.pallas_call(
        backward_kernel,
        out_shape=jax.ShapeDtypeStruct((8, TOKENS // 8, WIDTH), BF16),
        in_specs=[SMEM] + [VMEM] * (10 + len(SAVED)),
        out_specs=VMEM,
        scratch_shapes=[ROWS, GRADS],
        compiler_params=PARAMS,
        cost_estimate=pl.CostEstimate(
            flops=2 * TOKENS * WIDTH * 2560, bytes_accessed=18 << 20, transcendentals=0
        ),
        name="second_backward",
    )(
        info, *blocks, taps_inner, taps_state, rate, *in_vmem(turned[1:]), *in_vmem(saved)
    )


def pack_kernel(saved, cotangent, first, second, sems):
    copies = [
        pltpu.make_async_copy(saved.at[0, 0:1], first.at[0:1], sems.at[0]),
        pltpu.make_async_copy(cotangent, first.at[1:2], sems.at[1]),
        pltpu.make_async_copy(saved.at[0, 1:2], second, sems.at[2]),
    ]
    for copy in copies:
        copy.start()
    for copy in copies:
        copy.wait()


def pack_call(saved, cotangent):
    rows = cotangent.shape[1:]
    return pl.pallas_call(
        pack_kernel,
        out_shape=[jax.ShapeDtypeStruct((n,) + rows, BF16) for n in (2, 1)],
        in_specs=[HBM] * 2,
        out_specs=[VMEM] * 2,
        scratch_shapes=[pltpu.SemaphoreType.DMA((3,))],
        compiler_params=PARAMS,
        name="pack",
    )(*in_hbm([saved, cotangent]))


def merge_kernel(info, *refs):
    parts, (own, other, gain, loss, out) = refs[:4], refs[4:]
    for i, block in enumerate((own, other)):
        x = block[0].astype(F32)
        scale = row_scale(x)
        d_normed = sum(part[i].astype(F32) for part in parts)
        weighted = d_normed * gain[...]
        mean = jnp.mean(x * weighted, axis=-1, keepdims=True)
        back = scale * weighted - x * (scale * scale * scale) * mean
        if i == 0:
            back = back + own[1].astype(F32)
        out[i] = back.astype(BF16)

    @pl.when((info[0] >= 8) & (info[0] < 16))
    def _():
        out[0] = loss[...]


def merge_call(info, parts, own, other, gain, loss):
    return pl.pallas_call(
        merge_kernel,
        out_shape=jax.ShapeDtypeStruct(PAIR, BF16),
        in_specs=[SMEM] + [VMEM] * 8,
        out_specs=VMEM,
        compiler_params=PARAMS,
        name="merge",
    )(info, *parts, own, other, gain, loss)


def join_kernel(*refs):
    for step in range(4):
        refs[4][step] = refs[step][0]


def join_call(*blocks):
    return pl.pallas_call(
        join_kernel,
        out_shape=jax.ShapeDtypeStruct((4,) + PAIR[1:], BF16),
        in_specs=[VMEM] * 4,
        out_specs=VMEM,
        compiler_params=PARAMS,
        name="join",
    )(*blocks)


def pair_kernel(info, own, other, loss, out, rows):
    total = (own[0].astype(F32) + other[1].astype(F32)).astype(BF16)
    out[0] = total
    rows[0] = total
    out[1] = (own[1].astype(F32) + other[0].astype(F32)).astype(BF16)

    @pl.when(info[0] >= 16)
    def _():
        out[0] = loss[...]
        rows[0] = loss[...]
        out[1] = other[0]


def pair_call(info, own, other, loss):
    return pl.pallas_call(
        pair_kernel,
        out_shape=[jax.ShapeDtypeStruct(shape, BF16) for shape in (PAIR, (1,) + PAIR[1:])],
        in_specs=[SMEM] + [VMEM] * 3,
        out_specs=[VMEM] * 2,
        compiler_params=PARAMS,
        name="pair",
    )(info, own, other, loss)


def finish_kernel(parts, saved, grad_ref, gain_ref, out):
    x = saved[0, 1].astype(F32)
    scale = row_scale(x)
    d_normed = jnp.sum(parts[...].astype(F32), axis=0)
    weighted = d_normed * gain_ref[...]
    mean = jnp.mean(x * weighted, axis=-1, keepdims=True)
    back = scale * weighted - x * (scale * scale * scale) * mean
    out[0] = (grad_ref[0].astype(F32) + back).astype(BF16)


def finish_call(parts, saved, grad, gain):
    return pl.pallas_call(
        finish_kernel,
        out_shape=jax.ShapeDtypeStruct(grad.shape, BF16),
        in_specs=[VMEM] * 4,
        out_specs=VMEM,
        compiler_params=PARAMS,
        name="finish",
    )(parts, saved, grad, gain)


def exchange(blocks):
    return lax.all_to_all(blocks, "tensor", 0, 0)


def to_pair(values):
    count = lax.axis_size("tensor")
    return lax.ppermute(values, "tensor", [(i, i ^ 1) for i in range(count)])


def step_ahead(block, step):
    count = lax.axis_size("tensor")
    return lax.ppermute(block, "tensor", [(i, (i + 2 * step) % count) for i in range(count)])


def around(block):
    moved = {step: step_ahead(block, step) for step in (1, 3, 2)}
    return [block, moved[1], moved[2], moved[3]]


def pass_back(values, flip):
    sections, count = lax.axis_size("pipe"), lax.axis_size("tensor")
    route = [
        ((i + 1) % sections * count + j, i * count + (j ^ (1 if i == sections - 1 else flip)))
        for i in range(sections)
        for j in range(count)
    ]
    return lax.ppermute(values, ("pipe", "tensor"), route)


def per_device(
    saved,
    cotangent,
    loss_grad,
    lengths,
    gain,
    w_query,
    w_key,
    w_value,
    w_attn_out,
    w_inner,
    w_gate,
    w_state,
    w_step,
    w_mamba_out,
    conv_inner,
    conv_state,
    step_bias,
    decay_rate,
):
    wstep = w_step[0].T
    small = (gain, conv_inner[0], conv_state[0], step_bias, decay_rate)
    weights = (
        w_query[0],
        w_key[0],
        w_value[0],
        w_inner[0],
        w_gate[0],
        w_state[0],
        w_attn_out[0],
        w_mamba_out[0],
    )
    place = lax.axis_index("pipe")
    is_first = (place == 0).astype(jnp.int32)
    is_last = (place == lax.axis_size("pipe") - 1).astype(jnp.int32)
    info = lax.axis_index("tensor").astype(jnp.int32) + 8 * is_first + 16 * is_last
    info = info.reshape(1)

    own, second = pack_call(saved, cotangent)
    other = to_pair(own)
    blocks = around(own)
    blocks += [other, step_ahead(other, 1), to_pair(blocks[2]), step_ahead(other, 3)]
    seconds = around(second)
    query, other = lax.optimization_barrier((weights[0], other))
    turned = turn_call(wstep, (query,) + weights[1:])
    parts = whole_call(info, lengths, blocks, small, turned)
    parts, seconds = lax.optimization_barrier((parts, seconds))
    second = join_call(*seconds)
    second_blocks = (second, to_pair(second))
    parts = [parts[0]] + [step_ahead(parts[step], step) for step in (1, 3, 2)]
    parts, second_blocks = lax.optimization_barrier((parts, second_blocks))
    merged = merge_call(info, parts, own, other, gain, loss_grad)
    own, other = pass_back(merged, 0), pass_back(merged, 1)
    held = forward_call(info, lengths, second_blocks, small, turned)
    grad_block, grad_rows = pair_call(info, own, other, loss_grad)
    far = step_ahead(grad_rows, 2)
    grad_blocks = (grad_block, step_ahead(grad_block, 1), step_ahead(grad_block, 3), far, to_pair(far))
    parts = exchange(backward_call(info, grad_blocks, small, turned, held))
    return finish_call(parts, saved, grad_rows, gain)


def solution(mesh):
    placed = (
        P("pipe", None, "tensor", None),
        P("pipe", "tensor", None),
        P("tensor", None),
        P("pipe", None),
        P("pipe", None),
        P("pipe", None, "tensor"),
        P("pipe", None, "tensor"),
        P("pipe", None, "tensor"),
        P("pipe", "tensor", None),
        P("pipe", None, "tensor"),
        P("pipe", None, "tensor"),
        P("pipe", None, None),
        P("pipe", None, "tensor"),
        P("pipe", "tensor", None),
        P("pipe", None, "tensor"),
        P("pipe", None, None),
        P("pipe", "tensor"),
        P("pipe", "tensor"),
    )
    return jax.shard_map(
        per_device, mesh=mesh, in_specs=placed, out_specs=P("pipe", "tensor", None), check_vma=False
    )
```

```python
import functools

import jax
import jax.numpy as jnp
from jax import lax
from jax.experimental import pallas as pl
from jax.experimental.pallas import tpu as pltpu
from jax.sharding import PartitionSpec as P

HEAD_SIZE = 128
MAMBA_HEAD = 64
STATE_SIZE = 128
TOKENS = 128
WIDTH = 2560
LANES = 128
F32 = jnp.float32
BF16 = jnp.bfloat16
HIGHEST = lax.Precision.HIGHEST

NN = (((1,), (0,)), ((), ()))
NT = (((1,), (1,)), ((), ()))
TN = (((0,), (0,)), ((), ()))

QUERY, KEY, VALUE, INNER, GATE, STATE = (
    (0, 256),
    (256, 128),
    (384, 128),
    (512, 512),
    (1024, 512),
    (1536, 256),
)
GROUPS = (QUERY, KEY, VALUE, INNER, GATE, STATE)
JOINED = 1792
PADDED = 1920
ATTN_ROWS = 256
MAMBA_ROWS = 512
PAIRS = 4
HEADS = 8


def dot(a, b, dims=NN, precision=None):
    return lax.dot_general(a, b, dims, precision=precision, preferred_element_type=F32)


def dot_split(a, b, exact, pieces):
    rest = b if exact == 0 else a
    total = 0.0
    for _ in range(pieces):
        part = rest.astype(BF16)
        rest = rest - part.astype(F32)
        total = total + (dot(a, part) if exact == 0 else dot(part, b))
    return total


def iota(shape, axis):
    return lax.broadcasted_iota(jnp.int32, shape, axis)


def conv_forward(values, taps):
    rows = iota(values.shape, 0)
    total = values * taps[3:4]
    for lag in (1, 2, 3):
        moved = jnp.where(rows >= lag, pltpu.roll(values, lag, 0), 0.0)
        total = total + moved * taps[3 - lag : 4 - lag]
    return total


def conv_backward(grads, taps):
    count = grads.shape[0]
    rows = iota(grads.shape, 0)
    total = grads * taps[3:4]
    for lag in (1, 2, 3):
        moved = jnp.where(rows < count - lag, pltpu.roll(grads, count - lag, 0), 0.0)
        total = total + moved * taps[3 - lag : 4 - lag]
    return total


def silu_parts(u):
    gate = jax.nn.sigmoid(u)
    value = u * gate
    return value, gate * (1.0 + u * (1.0 - gate))


def widened(row):
    return jnp.concatenate([row, jnp.zeros((1, LANES - row.shape[1]), F32)], axis=1)


def low_lanes():
    return iota((TOKENS, LANES), 1) < MAMBA_HEAD


def tile_of(j):
    return slice(j * LANES, (j + 1) * LANES)


def forward(normed, wcat, length, taps_inner, taps_state, bias, rate, save):
    def project(group, more=0):
        start, size = group[0], group[1] + more
        return dot(normed, wcat[:, start : start + size])

    query = project(QUERY).astype(BF16)
    key = project(KEY).astype(BF16)
    value = project(VALUE).astype(BF16)
    stacked = jnp.concatenate([query[:, :HEAD_SIZE], query[:, HEAD_SIZE:]], axis=0)
    save["query"][...] = stacked
    save["key"][...] = key
    save["value"][...] = value
    scores = dot(stacked, key, NT) * HEAD_SIZE ** (-0.5)
    row = iota(scores.shape, 0)
    row = jnp.where(row >= TOKENS, row - TOKENS, row)
    place = iota(scores.shape, 1)
    scores = jnp.where((place <= row) & (place < length), scores, -1e30)
    expo = jnp.exp(scores - jnp.max(scores, axis=-1, keepdims=True))
    save["probs"][...] = expo / jnp.sum(expo, axis=-1, keepdims=True)

    projected = project(STATE, LANES)
    raw = projected[:, 2 * STATE_SIZE :] + widened(bias)
    step = jnp.maximum(raw, 0.0) + jnp.log1p(jnp.exp(-jnp.abs(raw)))
    earlier = iota((TOKENS, TOKENS), 1) <= iota((TOKENS, TOKENS), 0)
    total = dot_split(earlier.astype(BF16), -step * widened(rate), 0, 3)
    save["step"][...] = step
    save["step_slope"][...] = jax.nn.sigmoid(raw)
    total_rows = total.T

    states, slope = silu_parts(conv_forward(projected[:, : 2 * STATE_SIZE], taps_state))
    save["state_slope"][...] = slope
    b_in = states[:, :STATE_SIZE]
    c_out = states[:, STATE_SIZE:]
    save["states"][...] = states.astype(BF16)
    both = dot(c_out, b_in, NT, HIGHEST)

    inner = project(INNER).astype(BF16).astype(F32)
    mixed, slope = silu_parts(conv_forward(inner, taps_inner))
    save["mixed"][...] = mixed
    save["inner_slope"][...] = slope
    gate = project(GATE).astype(BF16).astype(F32)
    gated, slope = silu_parts(gate)
    save["gate"][...] = gated

    low = low_lanes()
    for j in range(PAIRS):
        at = tile_of(j)
        stepped = [step[:, h : h + 1] for h in (2 * j, 2 * j + 1)]
        steps = jnp.where(
            low,
            jnp.broadcast_to(stepped[0], (TOKENS, LANES)),
            jnp.broadcast_to(stepped[1], (TOKENS, LANES)),
        )
        scaled = (mixed[:, at] * steps).astype(BF16)
        save["steps"][:, at] = steps
        save["scaled"][:, at] = scaled
        parts = []
        for h in (2 * j, 2 * j + 1):
            diffs = total[:, h : h + 1] - total_rows[h : h + 1, :]
            decay = jnp.exp(jnp.where(earlier, diffs, -1e30))
            kernel = (both * decay).astype(BF16)
            save["decay"][:, h * LANES : (h + 1) * LANES] = decay
            save["kernel"][:, h * LANES : (h + 1) * LANES] = kernel
            parts.append(dot(kernel, scaled))
        summed = jnp.where(low, parts[0], parts[1])
        save["summed"][:, at] = summed
        save["gate_slope"][:, at] = (summed + mixed[:, at]) * slope[:, at]


def backward(grad, wout, wback, taps_inner, taps_state, rate, save, joined, out):
    d_attended = dot(grad, wout[:, :ATTN_ROWS]).astype(BF16)
    stacked = jnp.concatenate([d_attended[:, :HEAD_SIZE], d_attended[:, HEAD_SIZE:]], axis=0)
    probs = save["probs"][...]
    d_probs = dot(stacked, save["value"][...], NT).astype(BF16).astype(F32)
    weighted = probs * d_probs
    d_scores = weighted - probs * jnp.sum(weighted, axis=-1, keepdims=True)
    d_scores = (d_scores * HEAD_SIZE ** (-0.5)).astype(BF16)
    d_query = dot(d_scores, save["key"][...]).astype(BF16)
    joined[:, 0:HEAD_SIZE] = d_query[:TOKENS]
    joined[:, HEAD_SIZE : 2 * HEAD_SIZE] = d_query[TOKENS:]
    joined[:, 256:384] = dot(d_scores, save["query"][...], TN).astype(BF16)
    joined[:, 384:512] = dot(probs.astype(BF16), stacked, TN).astype(BF16)

    d_gated = dot(grad, wout[:, ATTN_ROWS:]).astype(BF16).astype(F32)
    joined[:, 1024:1536] = (d_gated * save["gate_slope"][...]).astype(BF16)
    d_scan = d_gated * save["gate"][...]
    d_scan_low = d_scan.astype(BF16)
    low = low_lanes()
    d_both = jnp.zeros((TOKENS, TOKENS), F32)
    d_mixed = []
    decay_terms = []
    step_terms = []
    for j in range(PAIRS):
        at = tile_of(j)
        tile = d_scan_low[:, at]
        scaled = save["scaled"][:, at]
        parts = []
        for i in (0, 1):
            h = 2 * j + i
            heads = slice(h * LANES, (h + 1) * LANES)
            own = jnp.where(low if i == 0 else jnp.logical_not(low), tile, jnp.zeros_like(tile))
            d_both = d_both + dot(own, scaled, NT) * save["decay"][:, heads]
            parts.append(dot(save["kernel"][:, heads], tile, TN))
        pulled = jnp.where(low, parts[0], parts[1])
        d_mixed.append(save["steps"][:, at] * pulled + d_scan[:, at])
        decay_terms.append(d_scan[:, at] * save["summed"][:, at])
        step_terms.append(save["mixed"][:, at] * pulled)
    d_mixed = jnp.concatenate(d_mixed, axis=1)
    d_inner = conv_backward(d_mixed * save["inner_slope"][...], taps_inner)
    joined[:, 512:1024] = d_inner.astype(BF16)

    d_both = d_both.astype(BF16)
    d_b = dot(d_both, save["states"][:, STATE_SIZE:], TN)
    d_c = dot(d_both, save["states"][:, :STATE_SIZE])
    d_states = jnp.concatenate([d_b, d_c], axis=1) * save["state_slope"][...]
    joined[:, 1536:1792] = conv_backward(d_states, taps_state).astype(BF16)

    shape = (MAMBA_ROWS, LANES)
    pick = (iota(shape, 0) // MAMBA_HEAD == iota(shape, 1)).astype(BF16)
    by_decay = dot_split(jnp.concatenate(decay_terms, axis=1), pick, 1, 2)
    by_step = dot_split(jnp.concatenate(step_terms, axis=1), pick, 1, 2)
    d_total = by_decay - save["step"][...] * by_step
    later = iota((TOKENS, TOKENS), 1) >= iota((TOKENS, TOKENS), 0)
    d_log = dot_split(later.astype(BF16), d_total, 0, 3)
    d_raw = (by_step - widened(rate) * d_log) * save["step_slope"][...]
    joined[:, JOINED:] = d_raw.astype(BF16)

    size = WIDTH // len(WBACK)
    for part in WBACK:
        lanes = slice(part * size, (part + 1) * size)
        total = dot(joined[...], wback[part]).astype(out.dtype)
        out[:, : TOKENS // 8, lanes] = total.reshape(8, TOKENS // 8, size)


WBACK = (0, 1, 2, 3, 4)
SAVED = {
    "query": ((2 * TOKENS, HEAD_SIZE), BF16),
    "key": ((TOKENS, HEAD_SIZE), BF16),
    "value": ((TOKENS, HEAD_SIZE), BF16),
    "probs": ((2 * TOKENS, TOKENS), F32),
    "step": ((TOKENS, LANES), F32),
    "step_slope": ((TOKENS, LANES), F32),
    "states": ((TOKENS, 2 * STATE_SIZE), BF16),
    "state_slope": ((TOKENS, 2 * STATE_SIZE), F32),
    "mixed": ((TOKENS, MAMBA_ROWS), F32),
    "inner_slope": ((TOKENS, MAMBA_ROWS), F32),
    "gate": ((TOKENS, MAMBA_ROWS), F32),
    "gate_slope": ((TOKENS, MAMBA_ROWS), F32),
    "steps": ((TOKENS, MAMBA_ROWS), F32),
    "scaled": ((TOKENS, MAMBA_ROWS), BF16),
    "summed": ((TOKENS, MAMBA_ROWS), F32),
    "decay": ((TOKENS, HEADS * LANES), F32),
    "kernel": ((TOKENS, HEADS * LANES), BF16),
}
N_IN = len(GROUPS)


def row_scale(x):
    return lax.rsqrt(jnp.mean(x * x, axis=-1, keepdims=True) + 1e-05)


def normalized(x_ref, gain_ref):
    x = x_ref[...].reshape(TOKENS, WIDTH).astype(F32)
    return (x * row_scale(x) * gain_ref[...]).astype(BF16)


def turn_kernel(wstep_from, *refs):
    sources = refs[: N_IN + 2]
    wcat, turned, wback, wout, wstep, sems = refs[N_IN + 2 :]
    load_step = pltpu.make_async_copy(wstep_from, wstep, sems.at[N_IN + 3])
    load_step.start()
    size = WIDTH // len(WBACK)
    loads = []
    for i, (start, columns) in enumerate(GROUPS):
        target = wcat.at[:, start : start + columns]
        loads.append(pltpu.make_async_copy(sources[i], target, sems.at[i]))
    for i, (source, start) in enumerate(((N_IN, 0), (N_IN + 1, 0), (N_IN + 1, 256))):
        rows = slice(256 * i, 256 * (i + 1))
        piece = sources[source].at[start : start + 256]
        loads.append(pltpu.make_async_copy(piece, wout.at[rows], sems.at[N_IN + i]))
    order = (3, 4, 7, 8, 6, 0, 5, 1, 2)
    for i in order:
        loads[i].start()
    wback[:, JOINED:, :] = jnp.zeros((len(WBACK), PADDED - JOINED, size), BF16)
    load_step.wait()
    for part in WBACK:
        wback[part, JOINED : JOINED + 16, :] = jnp.concatenate(
            [wstep[:, part * size : (part + 1) * size], jnp.zeros((8, size), BF16)], axis=0
        )
        block = wback[part, JOINED:, :]
        wcat[part * size : (part + 1) * size, JOINED:] = block.T
    for i in order:
        loads[i].wait()
        if i < N_IN:
            start, columns = GROUPS[i]
            for part in WBACK:
                block = wcat[part * size : (part + 1) * size, start : start + columns]
                wback[part, start : start + columns, :] = block.T
        else:
            rows = slice(256 * (i - N_IN), 256 * (i - N_IN + 1))
            turned[:, rows] = wout[rows, :].T


def place(me, blocks, lanes_of):
    for step in range(4):
        owner = lax.rem(me + 8 - 2 * step, 8)
        pair = owner + 1 - 2 * lax.rem(owner, 2)
        for index, target in lanes_of:
            target[owner] = blocks[step][index]
            target[pair] = blocks[4 + step][index]


def whole_kernel(info, lengths, *refs):
    blocks, refs = refs[:8], refs[8:]
    gain, taps_inner, taps_state, bias, rate = refs[:5]
    wcat, wout, wback = refs[5:8]
    outs = refs[8:12]
    x, grad, total, joined = refs[12:16]
    save = dict(zip(SAVED, refs[16:]))
    me = lax.rem(info[0], 8)
    place(me, blocks, ((0, x), (1, grad)))
    taps_i = taps_inner[...].astype(F32)
    taps_s = taps_state[...].astype(F32)
    forward(
        normalized(x, gain),
        wcat,
        lengths[0, 0],
        taps_i,
        taps_s,
        bias[...],
        rate[...],
        save,
    )
    backward(
        grad[...].reshape(TOKENS, WIDTH),
        wout,
        wback,
        taps_i,
        taps_s,
        rate[...],
        save,
        joined,
        total,
    )
    for step, out in enumerate(outs):
        owner = lax.rem(me + 2 * step, 8)
        out[0] = total[owner]
        out[1] = total[owner + 1 - 2 * lax.rem(owner, 2)]


def forward_kernel(info, lengths, *refs):
    own, other, refs = refs[0], refs[1], refs[2:]
    gain, taps_inner, taps_state, bias, rate, wcat = refs[:6]
    save = dict(zip(SAVED, refs[6 : 6 + len(SAVED)]))
    x = refs[6 + len(SAVED)]
    quarters = [block.at[i : i + 1] for block in (own, other) for i in range(4)]
    place(lax.rem(info[0], 8), quarters, ((0, x),))
    forward(
        normalized(x, gain),
        wcat,
        lengths[0, 1],
        taps_inner[...].astype(F32),
        taps_state[...].astype(F32),
        bias[...],
        rate[...],
        save,
    )


def backward_kernel(info, *refs):
    (block, next_one, last_one, far, far_pair), refs = refs[:5], refs[5:]
    taps_inner, taps_state, rate, wout, wback = refs[:5]
    save = dict(zip(SAVED, refs[5 : 5 + len(SAVED)]))
    out, grad, joined = refs[5 + len(SAVED) :]
    halves = [
        own
        for i, apart in enumerate((far, far_pair))
        for own in (block.at[i : i + 1], next_one.at[i : i + 1], apart, last_one.at[i : i + 1])
    ]
    place(lax.rem(info[0], 8), halves, ((0, grad),))
    backward(
        grad[...].reshape(TOKENS, WIDTH),
        wout,
        wback,
        taps_inner[...].astype(F32),
        taps_state[...].astype(F32),
        rate[...],
        save,
        joined,
        out,
    )


VMEM = pl.BlockSpec(memory_space=pltpu.VMEM)
SMEM = pl.BlockSpec(memory_space=pltpu.SMEM)
HBM = pl.BlockSpec(memory_space=pltpu.HBM)
WCAT_SHAPE = (WIDTH, PADDED)
WOUT_SHAPE = (WIDTH, ATTN_ROWS + MAMBA_ROWS)
WBACK_SHAPE = (len(WBACK), PADDED, WIDTH // len(WBACK))
GRADS = pltpu.VMEM((TOKENS, PADDED), BF16)
HELD = [pltpu.VMEM(shape, dtype) for shape, dtype in SAVED.values()]
ROWS = pltpu.VMEM((8, TOKENS // 8, WIDTH), BF16)
PARAMS = pltpu.CompilerParams(vmem_limit_bytes=16 * 1024 * 1024)


def in_hbm(arrays):
    return [pltpu.with_memory_space_constraint(array, pltpu.HBM) for array in arrays]


def in_vmem(arrays):
    return [pltpu.with_memory_space_constraint(array, pltpu.VMEM) for array in arrays]


def turn_call(wstep, weights):
    return pl.pallas_call(
        turn_kernel,
        out_shape=[pltpu.VMEM(s, BF16) for s in (WCAT_SHAPE, WOUT_SHAPE, WBACK_SHAPE)],
        in_specs=[HBM] * (N_IN + 3),
        out_specs=[VMEM] * 3,
        scratch_shapes=[
            pltpu.VMEM((ATTN_ROWS + MAMBA_ROWS, WIDTH), BF16),
            pltpu.VMEM((HEADS, WIDTH), BF16),
            pltpu.SemaphoreType.DMA((N_IN + 4,)),
        ],
        compiler_params=PARAMS,
        cost_estimate=pl.CostEstimate(flops=0, bytes_accessed=26 << 20, transcendentals=0),
        name="turn_weights",
    )(*in_hbm([wstep]), *in_hbm(weights))


PAIR = (2, TOKENS // 8, WIDTH)


def whole_call(info, lengths, blocks, small, turned):
    return pl.pallas_call(
        whole_kernel,
        out_shape=[jax.ShapeDtypeStruct(PAIR, BF16)] * 4,
        in_specs=[SMEM] * 2 + [VMEM] * 16,
        out_specs=[VMEM] * 4,
        scratch_shapes=[ROWS, ROWS, ROWS, GRADS] + HELD,
        compiler_params=PARAMS,
        cost_estimate=pl.CostEstimate(
            flops=2 * TOKENS * WIDTH * 4352, bytes_accessed=24 << 20, transcendentals=1 << 19
        ),
        name="section",
    )(info, lengths, *blocks, *small, *in_vmem(turned))


def forward_call(info, lengths, blocks, small, turned):
    return pl.pallas_call(
        forward_kernel,
        out_shape=[pltpu.VMEM(shape, dtype) for shape, dtype in SAVED.values()],
        in_specs=[SMEM] * 2 + [VMEM] * 8,
        out_specs=[VMEM] * len(SAVED),
        scratch_shapes=[ROWS],
        compiler_params=PARAMS,
        cost_estimate=pl.CostEstimate(
            flops=2 * TOKENS * WIDTH * 1800, bytes_accessed=13 << 20, transcendentals=1 << 19
        ),
        name="second_forward",
    )(info, lengths, *blocks, *small, *in_vmem(turned[:1]))


def backward_call(info, blocks, small, turned, saved):
    gain, taps_inner, taps_state, bias, rate = small
    return pl.pallas_call(
        backward_kernel,
        out_shape=jax.ShapeDtypeStruct((8, TOKENS // 8, WIDTH), BF16),
        in_specs=[SMEM] + [VMEM] * (10 + len(SAVED)),
        out_specs=VMEM,
        scratch_shapes=[ROWS, GRADS],
        compiler_params=PARAMS,
        cost_estimate=pl.CostEstimate(
            flops=2 * TOKENS * WIDTH * 2560, bytes_accessed=18 << 20, transcendentals=0
        ),
        name="second_backward",
    )(
        info, *blocks, taps_inner, taps_state, rate, *in_vmem(turned[1:]), *in_vmem(saved)
    )


def pack_kernel(saved, cotangent, out, first, sems):
    copies = [
        pltpu.make_async_copy(saved.at[0, 0:1], first.at[0:1], sems.at[0]),
        pltpu.make_async_copy(cotangent, first.at[1:2], sems.at[1]),
        pltpu.make_async_copy(saved.at[0, 0:1], out.at[0:1], sems.at[2]),
        pltpu.make_async_copy(cotangent, out.at[1:2], sems.at[3]),
        pltpu.make_async_copy(saved.at[0, 1:2], out.at[2:3], sems.at[4]),
    ]
    for copy in copies:
        copy.start()
    for copy in copies:
        copy.wait()


def pack_call(saved, cotangent):
    return pl.pallas_call(
        pack_kernel,
        out_shape=[jax.ShapeDtypeStruct((n,) + PAIR[1:], BF16) for n in (3, 2)],
        in_specs=[HBM] * 2,
        out_specs=[VMEM] * 2,
        scratch_shapes=[pltpu.SemaphoreType.DMA((5,))],
        compiler_params=PARAMS,
        name="pack",
    )(*in_hbm([saved, cotangent]))


def merge_kernel(info, *refs):
    parts, (own, other, gain, loss, out) = refs[:4], refs[4:]
    for i, block in enumerate((own, other)):
        x = block[0].astype(F32)
        scale = row_scale(x)
        d_normed = sum(part[i].astype(F32) for part in parts)
        weighted = d_normed * gain[...]
        mean = jnp.mean(x * weighted, axis=-1, keepdims=True)
        back = scale * weighted - x * (scale * scale * scale) * mean
        if i == 0:
            back = back + own[1].astype(F32)
        out[i] = back.astype(BF16)

    @pl.when((info[0] >= 8) & (info[0] < 16))
    def _():
        out[0] = loss[...]


def merge_call(info, parts, own, other, gain, loss):
    return pl.pallas_call(
        merge_kernel,
        out_shape=jax.ShapeDtypeStruct(PAIR, BF16),
        in_specs=[SMEM] + [VMEM] * 8,
        out_specs=VMEM,
        compiler_params=PARAMS,
        name="merge",
    )(info, *parts, own, other, gain, loss)


def join_kernel(*refs):
    for step in range(4):
        refs[4][step] = refs[step][2]


def join_call(*blocks):
    return pl.pallas_call(
        join_kernel,
        out_shape=jax.ShapeDtypeStruct((4,) + PAIR[1:], BF16),
        in_specs=[VMEM] * 4,
        out_specs=VMEM,
        compiler_params=PARAMS,
        name="join",
    )(*blocks)


def pair_kernel(info, own, other, loss, out, rows):
    total = (own[0].astype(F32) + other[1].astype(F32)).astype(BF16)
    out[0] = total
    rows[0] = total
    out[1] = (own[1].astype(F32) + other[0].astype(F32)).astype(BF16)

    @pl.when(info[0] >= 16)
    def _():
        out[0] = loss[...]
        rows[0] = loss[...]
        out[1] = other[0]


def pair_call(info, own, other, loss):
    return pl.pallas_call(
        pair_kernel,
        out_shape=[jax.ShapeDtypeStruct(shape, BF16) for shape in (PAIR, (1,) + PAIR[1:])],
        in_specs=[SMEM] + [VMEM] * 3,
        out_specs=[VMEM] * 2,
        compiler_params=PARAMS,
        name="pair",
    )(info, own, other, loss)


def finish_kernel(parts, saved, grad_ref, gain_ref, out):
    x = saved[0, 1].astype(F32)
    scale = row_scale(x)
    d_normed = jnp.sum(parts[...].astype(F32), axis=0)
    weighted = d_normed * gain_ref[...]
    mean = jnp.mean(x * weighted, axis=-1, keepdims=True)
    back = scale * weighted - x * (scale * scale * scale) * mean
    out[0] = (grad_ref[0].astype(F32) + back).astype(BF16)


def finish_call(parts, saved, grad, gain):
    return pl.pallas_call(
        finish_kernel,
        out_shape=jax.ShapeDtypeStruct(grad.shape, BF16),
        in_specs=[VMEM] * 4,
        out_specs=VMEM,
        compiler_params=PARAMS,
        name="finish",
    )(parts, saved, grad, gain)


def exchange(blocks):
    return lax.all_to_all(blocks, "tensor", 0, 0)


def to_pair(values):
    count = lax.axis_size("tensor")
    return lax.ppermute(values, "tensor", [(i, i ^ 1) for i in range(count)])


def step_ahead(block, step):
    count = lax.axis_size("tensor")
    return lax.ppermute(block, "tensor", [(i, (i + 2 * step) % count) for i in range(count)])


def around(block):
    moved = {step: step_ahead(block, step) for step in (1, 3, 2)}
    return [block, moved[1], moved[2], moved[3]]


def pass_back(values, flip):
    sections, count = lax.axis_size("pipe"), lax.axis_size("tensor")
    route = [
        ((i + 1) % sections * count + j, i * count + (j ^ (1 if i == sections - 1 else flip)))
        for i in range(sections)
        for j in range(count)
    ]
    return lax.ppermute(values, ("pipe", "tensor"), route)


def per_device(
    saved,
    cotangent,
    loss_grad,
    lengths,
    gain,
    w_query,
    w_key,
    w_value,
    w_attn_out,
    w_inner,
    w_gate,
    w_state,
    w_step,
    w_mamba_out,
    conv_inner,
    conv_state,
    step_bias,
    decay_rate,
):
    wstep = w_step[0].T
    small = (gain, conv_inner[0], conv_state[0], step_bias, decay_rate)
    weights = (
        w_query[0],
        w_key[0],
        w_value[0],
        w_inner[0],
        w_gate[0],
        w_state[0],
        w_attn_out[0],
        w_mamba_out[0],
    )
    place = lax.axis_index("pipe")
    is_first = (place == 0).astype(jnp.int32)
    is_last = (place == lax.axis_size("pipe") - 1).astype(jnp.int32)
    info = lax.axis_index("tensor").astype(jnp.int32) + 8 * is_first + 16 * is_last
    info = info.reshape(1)

    own_all, own = pack_call(saved, cotangent)
    other = to_pair(own)
    blocks = around(own_all)
    seconds = blocks
    blocks = blocks + [other, step_ahead(other, 1), to_pair(blocks[2]), step_ahead(other, 3)]
    query, other = lax.optimization_barrier((weights[0], other))
    turned = turn_call(wstep, (query,) + weights[1:])
    parts = whole_call(info, lengths, blocks, small, turned)
    parts, seconds = lax.optimization_barrier((parts, seconds))
    second = join_call(*seconds)
    second_blocks = (second, to_pair(second))
    parts = [parts[0]] + [step_ahead(parts[step], step) for step in (1, 3, 2)]
    parts, second_blocks = lax.optimization_barrier((parts, second_blocks))
    merged = merge_call(info, parts, own, other, gain, loss_grad)
    own, other = pass_back(merged, 0), pass_back(merged, 1)
    held = forward_call(info, lengths, second_blocks, small, turned)
    grad_block, grad_rows = pair_call(info, own, other, loss_grad)
    far = step_ahead(grad_rows, 2)
    grad_blocks = (grad_block, step_ahead(grad_block, 1), step_ahead(grad_block, 3), far, to_pair(far))
    parts = exchange(backward_call(info, grad_blocks, small, turned, held))
    return finish_call(parts, saved, grad_rows, gain)


def solution(mesh):
    placed = (
        P("pipe", None, "tensor", None),
        P("pipe", "tensor", None),
        P("tensor", None),
        P("pipe", None),
        P("pipe", None),
        P("pipe", None, "tensor"),
        P("pipe", None, "tensor"),
        P("pipe", None, "tensor"),
        P("pipe", "tensor", None),
        P("pipe", None, "tensor"),
        P("pipe", None, "tensor"),
        P("pipe", None, None),
        P("pipe", None, "tensor"),
        P("pipe", "tensor", None),
        P("pipe", None, "tensor"),
        P("pipe", None, None),
        P("pipe", "tensor"),
        P("pipe", "tensor"),
    )
    return jax.shard_map(
        per_device, mesh=mesh, in_specs=placed, out_specs=P("pipe", "tensor", None), check_vma=False
    )
```
